128 devices in a mesh: wa: 16 (over x, z), af: 8 (over y, core).
Axes of the slice: x: 4, y: 4, z: 4, core: 2. Of those that a mesh axis runs over, the one named last changes fastest.
Arguments:
- worker_ids: int32 [524288], P(('wa', 'af')), may hold values from 0 to 32767, as said below
- worker_attrs: bfloat16 [524288, 128], P(('wa', 'af')), may hold values from -16 to 16
- firm_ids: int32 [524288], P(('wa', 'af')), may hold values from 0 to 16383, as said below
- firm_attrs: bfloat16 [524288, 128], P(('wa', 'af')), may hold values from -16 to 16
- affinity: bfloat16 [128, 128], replicated, may hold values from -0.5 to 0.5
Outputs:
- worker_means: float32 [32768, 128], P('wa')
- firm_means: float32 [16384, 128], P('af')
- worker_potential: float32 [32768], P('wa')
- firm_potential: float32 [16384], P('af')
The draws below stay inside these ranges and needn't reach their ends.
Inputs may be any that keep to these rules, and one draw needn't show every extreme that they name: `worker_ids`: type ids come in blocks of 2048 consecutive worker types; in the rows of one device at most 512 records name one block, and in every device's rows some block is named by exactly 512. Counts per type are skewed and some types have no record. `firm_ids`: type ids come in blocks of 2048 consecutive firm types; in the rows of one device at most 1024 records name one block, and in every device's rows some block is named by exactly 1024. Counts per type are skewed and some types have no record.
All inputs are finite; a program needn't handle non-finite values.
Results may differ from the reference program's by a relative error of at most 0.00205.
The reference program's roundings to bfloat16 on the way (of `projected`) count: a program that leaves them out, or rounds other values in their place, can miss the bound.
Values may be sent and summed in bfloat16 or wider, within the bound.
No kernel may reach another device: no remote copies, remote signals or barrier semaphores. Data moves between devices by JAX's collectives and lax.ppermute only.
A program may use at most 64 MiB of HBM per device.

```python
import math
import jax
import jax.numpy as jnp
from jax import lax

W = 32768
F = 16384
K = 128
R_DEV = 4096
ITERS = 3
WT_DEV = 2048
FT_DEV = 2048
RECORDS = 524288
CAP_W = 512
CAP_F = 1024


def record_draw(key, salt, n_types, tile_types, capacity):
    key = jax.random.fold_in(key, salt)
    keys = jax.random.split(key, 7)
    groups = n_types // tile_types
    blocks = RECORDS // R_DEV
    heavy = jax.random.randint(keys[0], (blocks, 1), 0, groups)
    column = jnp.arange(R_DEV, dtype=jnp.int32)[None, :]
    spread = jnp.maximum(column - capacity, 0) % (groups - 1)
    owner = jnp.where(column < capacity, heavy, (heavy + 1 + spread) % groups)
    owner = jax.random.permutation(keys[1], owner, axis=1, independent=True)
    first = jax.random.randint(keys[2], (blocks, R_DEV), 0, tile_types)
    second = jax.random.randint(keys[3], (blocks, R_DEV), 0, tile_types)
    offset = jax.random.randint(keys[4], (groups,), 0, tile_types)
    slot = (jnp.minimum(first, second) + offset[owner]) % tile_types
    type_ids = (owner * tile_types + slot).reshape(RECORDS).astype(jnp.int32)
    centers = jax.random.normal(keys[5], (n_types, K), jnp.float32)
    noise = jax.random.normal(keys[6], (RECORDS, K), jnp.float32)
    return (type_ids, centers, noise)


def make_attrs(type_ids, centers, noise):
    scale = 0.5
    return jnp.clip(centers[type_ids] * scale + noise, -16.0, 16.0).astype(jnp.bfloat16)


def draw_worker_ids(key, part):
    type_ids, centers, noise = record_draw(key, 11, W, WT_DEV, CAP_W)
    return type_ids


def draw_worker_attrs(key, part):
    type_ids, centers, noise = record_draw(key, 11, W, WT_DEV, CAP_W)
    return make_attrs(type_ids, centers, noise)


def draw_firm_ids(key, part):
    type_ids, centers, noise = record_draw(key, 12, F, FT_DEV, CAP_F)
    return type_ids


def draw_firm_attrs(key, part):
    type_ids, centers, noise = record_draw(key, 12, F, FT_DEV, CAP_F)
    return make_attrs(type_ids, centers, noise)


def scatter_about(own_key, shape, scale, reach, kind=jnp.bfloat16):
    values = jax.random.normal(own_key, shape, jnp.float32) * scale
    return jnp.minimum(jnp.maximum(values, -reach), reach).astype(kind)


def setup_inputs(seed: int = 0) -> dict:
    key_list = jax.random.split(jax.random.key(seed), 6)
    worker_ids = draw_worker_ids(jax.random.fold_in(key_list[5], 71), 0)
    worker_attrs = draw_worker_attrs(jax.random.fold_in(key_list[5], 71), 0)
    firm_ids = draw_firm_ids(jax.random.fold_in(key_list[5], 71), 0)
    firm_attrs = draw_firm_attrs(jax.random.fold_in(key_list[5], 71), 0)
    affinity = scatter_about(key_list[4], (K, K), K ** -0.5, 0.5)
    return dict(worker_ids=worker_ids, worker_attrs=worker_attrs, firm_ids=firm_ids, firm_attrs=firm_attrs, affinity=affinity)


def type_means(attrs, type_ids, count):
    totals = jax.ops.segment_sum(attrs.astype(jnp.float32), type_ids, num_segments=count)
    tallies = jax.ops.segment_sum(jnp.ones(type_ids.shape, jnp.float32), type_ids, num_segments=count)
    return totals / jnp.maximum(tallies, 1.0)[:, None], tallies


def reference(worker_ids, worker_attrs, firm_ids, firm_attrs, affinity):
    worker_means, worker_tally = type_means(worker_attrs, worker_ids, W)
    firm_means, firm_tally = type_means(firm_attrs, firm_ids, F)
    log_worker = jnp.log(worker_tally + 1.0) - jnp.log(jnp.float32(RECORDS + W))
    log_firm = jnp.log(firm_tally + 1.0) - jnp.log(jnp.float32(RECORDS + F))
    projected = jnp.dot(worker_means.astype(jnp.bfloat16), affinity, preferred_element_type=jnp.float32).astype(jnp.bfloat16)
    projected = lax.optimization_barrier(projected).astype(jnp.float32)
    firm_rows = lax.optimization_barrier(firm_means.astype(jnp.bfloat16)).astype(jnp.float32)
    height = math.gcd(W, 512)
    stacked = projected.reshape(W // height, height, K)

    def surplus(rows_block):
        return jnp.dot(rows_block, firm_rows.T, precision=lax.Precision.HIGHEST, preferred_element_type=jnp.float32)

    firm_potential = jnp.zeros((F,), jnp.float32)
    worker_potential = jnp.zeros((W,), jnp.float32)
    for rounds in range(ITERS):
        def row_lse(rows_block, shift=firm_potential):
            scores = surplus(rows_block) + shift[None, :]
            peak = jnp.max(scores, axis=1)
            return peak + jnp.log(jnp.sum(jnp.exp(scores - peak[:, None]), axis=1))

        worker_potential = log_worker - lax.map(row_lse, stacked).reshape(W)

        def col_step(carry, inputs):
            peak, total = carry
            rows_block, shift_block = inputs
            scores = surplus(rows_block) + shift_block[:, None]
            new_peak = jnp.maximum(peak, jnp.max(scores, axis=0))
            total = total * jnp.exp(peak - new_peak) + jnp.sum(jnp.exp(scores - new_peak[None, :]), axis=0)
            return (new_peak, total), None

        start = (jnp.full((F,), -1e30, jnp.float32), jnp.zeros((F,), jnp.float32))
        (peak, total), unused = lax.scan(col_step, start, (stacked, worker_potential.reshape(W // height, height)))
        firm_potential = log_firm - (peak + jnp.log(total))
    return worker_means, firm_means, worker_potential, firm_potential
```

```python
import functools

import jax
import jax.numpy as jnp
from jax import lax
from jax.experimental import pallas as pl
from jax.experimental.pallas import tpu as pltpu
from jax.sharding import PartitionSpec as P

W = 32768
F = 16384
K = 128
ITERS = 3
TILE = 2048
LANES = 128
BLOCKS = TILE // LANES
ID_ROWS = 16
CHUNK = 256
UNROLL = 32
WIDE = 256
F32 = jnp.float32
BF16 = jnp.bfloat16

NT = (((1,), (1,)), ((), ()))
NN = (((1,), (0,)), ((), ()))


def _params(mib):
    return pltpu.CompilerParams(vmem_limit_bytes=mib << 20)


def _dot(a, b, dims=NN):
    return lax.dot_general(a, b, dims, preferred_element_type=F32)


def _flag(mask):
    return jnp.where(mask, 1.0, 0.0).astype(BF16)


def pack_kernel(groups, capacity, ids_ref, attrs_ref, out_ref, dest_v, dest_s, wide, placed, sem):
    rows = ids_ref.shape[0]
    ids = ids_ref[...]
    owner = lax.shift_right_logical(ids, 11)
    local = jnp.bitwise_and(ids, TILE - 1)
    sub = lax.broadcasted_iota(jnp.int32, (LANES, LANES), 0)
    lane = lax.broadcasted_iota(jnp.int32, (LANES, LANES), 1)
    before = _flag(sub < lane)
    every = jnp.ones((LANES, LANES), BF16)
    above = _flag(
        lax.broadcasted_iota(jnp.int32, (rows, rows), 1)
        < lax.broadcasted_iota(jnp.int32, (rows, rows), 0)
    )
    masks = [owner == g for g in range(groups)]
    stacked = jnp.concatenate([_flag(m) for m in masks], axis=0)
    inside = _dot(stacked, before)
    totals = _dot(stacked, every).astype(BF16)
    slot = jnp.zeros((rows, LANES), F32)
    for g in range(groups):
        part = slice(g * rows, (g + 1) * rows)
        slot = jnp.where(masks[g], inside[part] + _dot(above, totals[part]), slot)
    slot = slot.astype(jnp.int32)
    dest_v[...] = owner * capacity + slot
    to_scalar = pltpu.make_async_copy(dest_v, dest_s, sem)
    to_scalar.start()

    line = lax.shift_right_logical(slot, 7)
    column = jnp.bitwise_and(slot, LANES - 1)
    high_row = owner * ID_ROWS + line
    low_row = high_row + capacity // LANES
    high = (lax.shift_right_logical(local, 6) + 1).astype(F32)
    low = jnp.bitwise_and(local, 63).astype(F32)
    place = lax.broadcasted_iota(jnp.int32, (groups * ID_ROWS, LANES), 0)
    packed = jnp.zeros((groups * ID_ROWS, LANES), F32)
    for c in range(rows):
        r = slice(c, c + 1)
        values = jnp.where(place == high_row[r], high[r], 0.0) + jnp.where(
            place == low_row[r], low[r], 0.0
        )
        packed += _dot(values.astype(BF16), _flag(sub == column[r]), NT)
    packed = packed.astype(BF16)
    for g in range(groups):
        out_ref[g, capacity : capacity + ID_ROWS, :] = packed[g * ID_ROWS : (g + 1) * ID_ROWS]

    wide[...] = attrs_ref[...].astype(F32)
    placed[...] = jnp.zeros_like(placed)
    to_scalar.wait()

    @pl.loop(0, rows * LANES // UNROLL)
    def _(step):
        row = step // (LANES // UNROLL)
        first = (step % (LANES // UNROLL)) * UNROLL
        for u in range(UNROLL):
            to = dest_s[row, first + u]
            placed[pl.ds(to, 1), :] = wide[pl.ds(step * UNROLL + u, 1), :]

    @pl.loop(0, groups)
    def _(g):
        out_ref[g, 0:capacity, :] = placed[
            pl.ds(pl.multiple_of(g * capacity, capacity), capacity), :
        ].astype(BF16)


def pack(ids, attrs, groups):
    rows = ids.shape[0]
    capacity = 2 * rows // groups
    return pl.pallas_call(
        functools.partial(pack_kernel, groups, capacity),
        out_shape=jax.ShapeDtypeStruct((groups, capacity + ID_ROWS, K), BF16),
        in_specs=[pl.BlockSpec(memory_space=pltpu.VMEM)] * 2,
        out_specs=pl.BlockSpec(memory_space=pltpu.VMEM),
        scratch_shapes=[
            pltpu.VMEM((rows // LANES, LANES), jnp.int32),
            pltpu.SMEM((rows // LANES, LANES), jnp.int32),
            pltpu.VMEM((rows, K), F32),
            pltpu.VMEM((groups * capacity, K), F32),
            pltpu.SemaphoreType.DMA,
        ],
        compiler_params=_params(24),
        cost_estimate=pl.CostEstimate(flops=1 << 32, bytes_accessed=1 << 23, transcendentals=0),
        name="pack_records",
    )(ids.reshape(rows // LANES, LANES), attrs)


def pool_kernel(groups, capacity, parts, recv_ref, out_ref, sums, tallies):
    sums[...] = jnp.zeros_like(sums)
    tallies[...] = jnp.zeros_like(tallies)
    types = lax.broadcasted_iota(jnp.int32, (TILE, CHUNK), 0)
    lines = capacity // LANES
    wide = CHUNK // LANES

    @pl.loop(0, groups)
    def _(g):
        coded = recv_ref[g, capacity : capacity + ID_ROWS, :].astype(F32).astype(jnp.int32)
        for q in range(capacity // CHUNK):
            ids = jnp.concatenate(
                [
                    (coded[i : i + 1] - 1) * 64 + coded[lines + i : lines + i + 1]
                    for i in range(q * wide, (q + 1) * wide)
                ],
                axis=1,
            )

            @pl.when(jnp.max(ids) >= 0)
            def _():
                x = recv_ref[g, q * CHUNK : (q + 1) * CHUNK, :]
                sums[...] += _dot(_flag(types == ids), x)
                line = jnp.right_shift(ids, 7)
                column = jnp.bitwise_and(ids, LANES - 1)
                tallies[...] += _dot(
                    _flag(types[:BLOCKS] == line), _flag(types[:LANES] == column), NT
                )

    share = TILE // parts
    for k in range(parts):
        out_ref[k, 0:share, :] = sums[k * share : (k + 1) * share, :]
        out_ref[k, share : share + BLOCKS, :] = tallies[...]


def pool(recv, parts):
    groups, depth, width = recv.shape
    return pl.pallas_call(
        functools.partial(pool_kernel, groups, depth - ID_ROWS, parts),
        out_shape=jax.ShapeDtypeStruct((parts, TILE // parts + BLOCKS, K), F32),
        in_specs=[pl.BlockSpec(memory_space=pltpu.VMEM)],
        out_specs=pl.BlockSpec(memory_space=pltpu.VMEM),
        scratch_shapes=[pltpu.VMEM((TILE, K), F32), pltpu.VMEM((BLOCKS, LANES), F32)],
        compiler_params=_params(24),
        cost_estimate=pl.CostEstimate(flops=1 << 33, bytes_accessed=1 << 22, transcendentals=0),
        name="pool_records",
    )(recv)


def upright(row):
    return jnp.transpose(jnp.broadcast_to(row, (LANES, LANES)))


def mean_kernel(parts, me_ref, recv_ref, high_ref, low_ref, tally_ref):
    share = TILE // parts
    tally = recv_ref[0, share : share + BLOCKS, :]
    total = recv_ref[0, 0:share, :]
    for k in range(1, parts):
        tally += recv_ref[k, share : share + BLOCKS, :]
        total += recv_ref[k, 0:share, :]
    tally_ref[...] = tally
    me = me_ref[0]
    lines = share // LANES
    counts = jnp.concatenate(
        [upright(tally_ref[pl.ds(me * lines + i, 1), :]) for i in range(lines)], axis=0
    )
    means = total / jnp.maximum(counts, 1.0)
    high = means.astype(BF16)
    low = (means - high.astype(F32)).astype(BF16)
    for k in range(parts):
        high_ref[k] = high
        low_ref[k] = low


def mean_share(recv, axis):
    parts, depth, width = recv.shape
    share = TILE // parts
    me = lax.axis_index(axis).astype(jnp.int32).reshape(1)
    return pl.pallas_call(
        functools.partial(mean_kernel, parts),
        out_shape=(
            jax.ShapeDtypeStruct((parts, share, K), BF16),
            jax.ShapeDtypeStruct((parts, share, K), BF16),
            jax.ShapeDtypeStruct((BLOCKS, LANES), F32),
        ),
        in_specs=[
            pl.BlockSpec(memory_space=pltpu.SMEM),
            pl.BlockSpec(memory_space=pltpu.VMEM),
        ],
        out_specs=(pl.BlockSpec(memory_space=pltpu.VMEM),) * 3,
        compiler_params=_params(24),
        cost_estimate=pl.CostEstimate(flops=1 << 20, bytes_accessed=1 << 22, transcendentals=0),
        name="mean_share",
    )(me, recv)


def combine(recv_ref, mass_ref):
    peak = recv_ref[0]
    for k in range(1, recv_ref.shape[0]):
        peak = jnp.maximum(peak, recv_ref[k])
    total = jnp.exp(recv_ref[0] - peak)
    for k in range(1, recv_ref.shape[0]):
        total += jnp.exp(recv_ref[k] - peak)
    return mass_ref[...] - (peak + jnp.log(total))


def lse_over_rows(a_ref, b_ref, shift, scores, emit):
    for j in range(TILE // WIDE):
        slot = scores.at[j % 2]
        b = b_ref[j * WIDE : (j + 1) * WIDE, :]
        peak = None
        for t in range(TILE // WIDE):
            part = slice(t * WIDE, (t + 1) * WIDE)
            s = _dot(a_ref[part, :], b, NT)
            if shift is not None:
                moved = shift[part, :]
                s += jnp.concatenate([moved] * (WIDE // LANES), axis=1)
            slot[part, :] = s
            top = jnp.max(s.reshape(WIDE // 8, 8, WIDE), axis=0)
            peak = top if peak is None else jnp.maximum(peak, top)
        peak = jnp.max(peak, axis=0, keepdims=True)
        total = None
        for t in range(TILE // WIDE):
            part = slice(t * WIDE, (t + 1) * WIDE)
            e = jnp.exp(slot[part, :] - peak)
            e = jnp.sum(e.reshape(WIDE // 8, 8, WIDE), axis=0)
            total = e if total is None else total + e
        lse = peak + jnp.log(jnp.sum(total, axis=0, keepdims=True))
        for i in range(WIDE // LANES):
            emit(j * (WIDE // LANES) + i, lse[:, i * LANES : (i + 1) * LANES])


def first_kernel(means_ref, affinity_ref, firm_ref, out_ref, projected_ref, scores):
    projected_ref[...] = _dot(means_ref[...], affinity_ref[...]).astype(BF16)

    def emit(line, row):
        for k in range(out_ref.shape[0]):
            out_ref[k, line : line + 1, :] = row

    lse_over_rows(firm_ref, projected_ref, None, scores, emit)


def sweep_kernel(recv_ref, mass_ref, a_ref, b_ref, out_ref, pot_ref, shift, scores):
    pot_ref[...] = combine(recv_ref, mass_ref)
    for i in range(BLOCKS):
        shift[i * LANES : (i + 1) * LANES, :] = upright(pot_ref[i : i + 1, :])

    def emit(line, row):
        for k in range(out_ref.shape[0]):
            out_ref[k, line : line + 1, :] = row

    lse_over_rows(a_ref, b_ref, shift, scores, emit)


VM = pl.BlockSpec(memory_space=pltpu.VMEM)
SWEEP_COST = pl.CostEstimate(
    flops=2 * TILE * TILE * K, bytes_accessed=1 << 21, transcendentals=TILE * TILE
)


def first_pass(means, affinity, firm_rows, parts):
    return pl.pallas_call(
        first_kernel,
        out_shape=(
            jax.ShapeDtypeStruct((parts, BLOCKS, LANES), F32),
            jax.ShapeDtypeStruct((TILE, K), BF16),
        ),
        in_specs=[VM] * 3,
        out_specs=(VM, VM),
        scratch_shapes=[pltpu.VMEM((2, TILE, WIDE), F32)],
        compiler_params=_params(32),
        cost_estimate=SWEEP_COST,
        name="first_pass",
    )(means, affinity, firm_rows)


def sweep(recv, mass, a, b, parts):
    return pl.pallas_call(
        sweep_kernel,
        out_shape=(
            jax.ShapeDtypeStruct((parts, BLOCKS, LANES), F32),
            jax.ShapeDtypeStruct((BLOCKS, LANES), F32),
        ),
        in_specs=[VM] * 4,
        out_specs=(VM, VM),
        scratch_shapes=[pltpu.VMEM((TILE, LANES), F32), pltpu.VMEM((2, TILE, WIDE), F32)],
        compiler_params=_params(32),
        cost_estimate=SWEEP_COST,
        name="sweep_pass",
    )(recv, mass, a, b)


def last_kernel(recv_ref, mass_ref, pot_ref):
    pot_ref[...] = combine(recv_ref, mass_ref)


def last_pass(recv, mass):
    return pl.pallas_call(
        last_kernel,
        out_shape=jax.ShapeDtypeStruct((BLOCKS, LANES), F32),
        in_specs=[VM] * 2,
        out_specs=VM,
        compiler_params=_params(16),
        name="last_combine",
    )(recv, mass)


def swap(x, axis):
    return lax.all_to_all(x, axis, split_axis=0, concat_axis=0, tiled=True)


def body(worker_ids, worker_attrs, firm_ids, firm_attrs, affinity):
    wa_count = lax.axis_size("wa")
    af_count = lax.axis_size("af")
    records_all = worker_ids.shape[0] * wa_count * af_count

    worker_sent = pack(worker_ids, worker_attrs, wa_count)
    worker_recv = swap(worker_sent, "wa")
    firm_sent = pack(firm_ids, firm_attrs, af_count)
    firm_recv = swap(firm_sent, "af")
    worker_part = swap(pool(worker_recv, af_count), "af")
    firm_part = swap(pool(firm_recv, wa_count), "wa")
    worker_high, worker_low, worker_tally = mean_share(worker_part, "af")
    firm_high, firm_low, firm_tally = mean_share(firm_part, "wa")
    worker_high = swap(worker_high, "af").reshape(TILE, K)
    firm_high = swap(firm_high, "wa").reshape(TILE, K)

    log_worker = jnp.log(worker_tally + 1.0) - jnp.log(jnp.float32(records_all + W))
    log_firm = jnp.log(firm_tally + 1.0) - jnp.log(jnp.float32(records_all + F))

    partial, projected = first_pass(worker_high, affinity, firm_high, af_count)
    worker_low = swap(worker_low, "af").reshape(TILE, K)
    firm_low = swap(firm_low, "wa").reshape(TILE, K)
    worker_means = worker_high.astype(F32) + worker_low.astype(F32)
    firm_means = firm_high.astype(F32) + firm_low.astype(F32)
    for rounds in range(ITERS):
        partial, worker_potential = sweep(
            swap(partial, "af"), log_worker, projected, firm_high, wa_count
        )
        partial = swap(partial, "wa")
        if rounds < ITERS - 1:
            partial, unused = sweep(partial, log_firm, firm_high, projected, af_count)
    firm_potential = last_pass(partial, log_firm)
    return (worker_means, firm_means, worker_potential.reshape(TILE), firm_potential.reshape(TILE))


def solution(mesh):
    placed = (P(("wa", "af")), P(("wa", "af"), None), P(("wa", "af")), P(("wa", "af"), None), P())
    return jax.shard_map(
        body,
        mesh=mesh,
        in_specs=placed,
        out_specs=(P("wa", None), P("af", None), P("wa"), P("af")),
        check_vma=False,
    )
```

```python
import functools
import math

import jax
import jax.numpy as jnp
from jax import lax
from jax.experimental import pallas as pl
from jax.experimental.pallas import tpu as pltpu
from jax.sharding import PartitionSpec as P

W = 32768
F = 16384
K = 128
ITERS = 3
TILE = 2048
LANES = 128
BLOCKS = TILE // LANES
ID_ROWS = 16
CHUNK = 512
WIDE = 256
TINY = 1e-25
F32 = jnp.float32
BF16 = jnp.bfloat16

VM = pl.BlockSpec(memory_space=pltpu.VMEM)
SM = pl.BlockSpec(memory_space=pltpu.SMEM)
ANY = pl.BlockSpec(memory_space=pl.ANY)
HEAVY = pl.CostEstimate(flops=1 << 33, bytes_accessed=1 << 22, transcendentals=0)
LIGHT = pl.CostEstimate(flops=1 << 20, bytes_accessed=1 << 16, transcendentals=0)
NT = (((1,), (1,)), ((), ()))
NN = (((1,), (0,)), ((), ()))


def _params(mib):
    return pltpu.CompilerParams(vmem_limit_bytes=mib << 20)


def _dot(a, b, dims=NN):
    return lax.dot_general(a, b, dims, preferred_element_type=F32)


def _flag(mask):
    return jnp.where(mask, 1.0, 0.0).astype(BF16)


def pack_kernel(groups, capacity, me_ref, ids_ref, attrs_ref, after_ref, *rest):
    outs, (dest_v, dest_s, wide, placed, sem) = rest[:-5], rest[-5:]
    rows = ids_ref.shape[0]
    ids = ids_ref[...]
    owner = jnp.bitwise_xor(lax.shift_right_logical(ids, 11), me_ref[0])
    local = jnp.bitwise_and(ids, TILE - 1)
    sub = lax.broadcasted_iota(jnp.int32, (LANES, LANES), 0)
    lane = lax.broadcasted_iota(jnp.int32, (LANES, LANES), 1)
    before = _flag(sub < lane)
    every = jnp.ones((LANES, LANES), BF16)
    above = _flag(
        lax.broadcasted_iota(jnp.int32, (rows, rows), 1)
        < lax.broadcasted_iota(jnp.int32, (rows, rows), 0)
    )
    masks = [owner == g for g in range(groups)]
    stacked = jnp.concatenate([_flag(m) for m in masks], axis=0)
    inside = _dot(stacked, before)
    totals = _dot(stacked, every).astype(BF16)
    slot = jnp.zeros((rows, LANES), F32)
    for g in range(groups):
        part = slice(g * rows, (g + 1) * rows)
        slot = jnp.where(masks[g], inside[part] + _dot(above, totals[part]), slot)
    slot = slot.astype(jnp.int32)
    dest_v[...] = owner * capacity + slot
    to_scalar = pltpu.make_async_copy(dest_v, dest_s, sem)
    to_scalar.start()

    line = lax.shift_right_logical(slot, 7)
    column = jnp.bitwise_and(slot, LANES - 1)
    high_row = owner * ID_ROWS + line
    low_row = high_row + capacity // LANES
    high = (lax.shift_right_logical(local, 6) + 1).astype(F32)
    low = jnp.bitwise_and(local, 63).astype(F32)
    place = lax.broadcasted_iota(jnp.int32, (groups * ID_ROWS, LANES), 0)
    packed = jnp.zeros((groups * ID_ROWS, LANES), F32)
    for c in range(rows):
        r = slice(c, c + 1)
        values = jnp.where(place == high_row[r], high[r], 0.0) + jnp.where(
            place == low_row[r], low[r], 0.0
        )
        packed += _dot(values.astype(BF16), _flag(sub == column[r]), NT)
    packed = packed.astype(BF16)
    for g in range(groups):
        behind = packed[g * ID_ROWS : (g + 1) * ID_ROWS]
        if len(outs) == 1:
            outs[0][g, capacity : capacity + ID_ROWS, :] = behind
        else:
            outs[g][capacity : capacity + ID_ROWS, :] = behind

    wide[...] = attrs_ref[...].astype(F32)
    placed[...] = jnp.zeros_like(placed)
    to_scalar.wait()

    @pl.loop(0, rows)
    def _(row):
        first = pl.multiple_of(row * LANES, LANES)
        held = [wide[pl.ds(first + u, 1), :] for u in range(LANES)]
        to = [dest_s[row, u] for u in range(LANES)]
        for u in range(LANES):
            placed[pl.ds(to[u], 1), :] = held[u]

    for g in range(groups):
        group = placed[g * capacity : (g + 1) * capacity, :].astype(BF16)
        if len(outs) == 1:
            outs[0][g, 0:capacity, :] = group
        else:
            outs[g][0:capacity, :] = group


def pack(ids, attrs, groups, me, after):
    rows = ids.shape[0]
    capacity = 2 * rows // groups
    if me is None:
        me = jnp.zeros((1,), jnp.int32)
        made = (jax.ShapeDtypeStruct((groups, capacity + ID_ROWS, K), BF16),)
    else:
        made = (jax.ShapeDtypeStruct((capacity + ID_ROWS, K), BF16),) * groups
    return pl.pallas_call(
        functools.partial(pack_kernel, groups, capacity),
        out_shape=made,
        in_specs=[SM, VM, VM, ANY],
        out_specs=(VM,) * len(made),
        scratch_shapes=[
            pltpu.VMEM((rows // LANES, LANES), jnp.int32),
            pltpu.SMEM((rows // LANES, LANES), jnp.int32),
            pltpu.VMEM((rows, K), F32),
            pltpu.VMEM((groups * capacity, K), F32),
            pltpu.SemaphoreType.DMA,
        ],
        compiler_params=_params(24),
        cost_estimate=LIGHT,
        name="pack_records",
    )(me, ids.reshape(rows // LANES, LANES), attrs, after)


def pool_kernel(groups, capacity, split, me_ref, after_ref, *rest):
    recvs, outs, (sums, tallies, more) = rest[: -split - 3], rest[-split - 3 : -3], rest[-3:]
    if len(recvs) == 1:
        recvs = [recvs[0].at[g] for g in range(groups)]
    half = capacity // 2
    lines = capacity // LANES
    types = lax.broadcasted_iota(jnp.int32, (TILE, CHUNK), 0)

    def ids_of(recv, begin, end):
        coded = recv[capacity : capacity + ID_ROWS, :].astype(F32).astype(jnp.int32)
        return [
            (coded[i : i + 1] - 1) * 64 + coded[lines + i : lines + i + 1]
            for i in range(begin, end)
        ]

    def add(ids, x, fresh=False):
        ids = jnp.concatenate(ids, axis=1)
        wide = ids.shape[1]
        total = _dot(_flag(types[:, :wide] == ids), x)
        line = jnp.right_shift(ids, 7)
        column = jnp.bitwise_and(ids, LANES - 1)
        tally = _dot(
            _flag(types[:BLOCKS, :wide] == line), _flag(types[:LANES, :wide] == column), NT
        )
        sums[...] = total if fresh else sums[...] + total
        tallies[...] = tally if fresh else tallies[...] + tally

    for g in range(groups):
        more[g] = jnp.max(
            recvs[g][capacity : capacity + ID_ROWS, :].astype(F32)[lines // 2 : lines]
        ).astype(jnp.int32)
    together = max(1, CHUNK // half)
    for g in range(0, groups, together):
        ids = [i for k in range(together) for i in ids_of(recvs[g + k], 0, lines // 2)]
        x = [recvs[g + k][0:half, :] for k in range(together)]
        add(ids, x[0] if together == 1 else jnp.concatenate(x, axis=0), g == 0)
    for g in range(groups):

        @pl.when(more[g] > 0)
        def _(recv=recvs[g]):
            add(ids_of(recv, lines // 2, lines), recv[half:capacity, :])

    if split == 1:
        parts = outs[0].shape[0]
        share = TILE // parts
        for k in range(parts):
            outs[0][k, 0:share, :] = sums[k * share : (k + 1) * share, :]
            outs[0][k, share : share + BLOCKS, :] = tallies[...]
    else:
        share = TILE // split
        for k in range(split):
            begin = pl.multiple_of(jnp.bitwise_xor(me_ref[0], k) * share, share)
            outs[k][0:share, :] = sums[pl.ds(begin, share), :]
            outs[k][share : share + BLOCKS, :] = tallies[...]


def pool(recvs, parts, me, after, cost):
    if len(recvs) == 1:
        groups, depth = recvs[0].shape[:2]
    else:
        groups, depth = len(recvs), recvs[0].shape[0]
    rows = TILE // parts + BLOCKS
    if me is None:
        me = jnp.zeros((1,), jnp.int32)
        made = (jax.ShapeDtypeStruct((parts, rows, K), F32),)
    else:
        made = (jax.ShapeDtypeStruct((rows, K), F32),) * parts
    return pl.pallas_call(
        functools.partial(pool_kernel, groups, depth - ID_ROWS, len(made)),
        out_shape=made,
        in_specs=[SM, ANY] + [VM] * len(recvs),
        out_specs=(VM,) * len(made),
        scratch_shapes=[
            pltpu.VMEM((TILE, K), F32),
            pltpu.VMEM((BLOCKS, LANES), F32),
            pltpu.SMEM((groups,), jnp.int32),
        ],
        compiler_params=_params(24),
        cost_estimate=cost,
        name="pool_records",
    )(me, after, *recvs)


def upright(row):
    return jnp.transpose(jnp.broadcast_to(row, (LANES, LANES)))


def mean_kernel(share, spread, behind, me_ref, *rest):
    recvs, (mean_ref, tally_ref) = rest[behind:-2], rest[-2:]
    if len(recvs) == 1:
        recvs = [recvs[0].at[k] for k in range(recvs[0].shape[0])]
    tally = recvs[0][share : share + BLOCKS, :]
    total = recvs[0][0:share, :]
    for recv in recvs[1:]:
        tally += recv[share : share + BLOCKS, :]
        total += recv[0:share, :]
    tally_ref[...] = tally
    me = me_ref[0]
    lines = share // LANES
    counts = jnp.concatenate(
        [upright(tally_ref[pl.ds(me * lines + i, 1), :]) for i in range(lines)], axis=0
    )
    means = total / jnp.maximum(counts, 1.0)
    if spread:
        for k in range(mean_ref.shape[0]):
            mean_ref[k] = means
    else:
        mean_ref[...] = means


def mean_share(recvs, me, spread, after):
    parts, depth = (recvs[0].shape[0] if len(recvs) == 1 else len(recvs)), recvs[0].shape[-2]
    share = depth - BLOCKS
    made = jax.ShapeDtypeStruct((parts, share, K) if spread else (share, K), F32)
    return pl.pallas_call(
        functools.partial(mean_kernel, share, spread, len(after)),
        out_shape=(made, jax.ShapeDtypeStruct((BLOCKS, LANES), F32)),
        in_specs=[SM] + [ANY] * len(after) + [VM] * len(recvs),
        out_specs=(VM,) * 2,
        compiler_params=_params(24),
        cost_estimate=LIGHT,
        name="mean_share",
    )(me, *after, *recvs)


def combine(recv_ref, tally_ref, mass):
    peak = recv_ref[0]
    for k in range(1, recv_ref.shape[0]):
        peak = jnp.maximum(peak, recv_ref[k])
    total = jnp.exp(recv_ref[0] - peak)
    for k in range(1, recv_ref.shape[0]):
        total += jnp.exp(recv_ref[k] - peak)
    return (jnp.log(tally_ref[...] + 1.0) - math.log(mass)) - (peak + jnp.log(total))


def spread_line(out_ref, line, row):
    for k in range(out_ref.shape[0]):
        out_ref[k, line : line + 1, :] = row


def exact_lse(a_far, b_far, pot_ref, shift, scores, a_ref, b_ref, sems, out_ref):
    copies = [
        pltpu.make_async_copy(a_far, a_ref, sems.at[0]),
        pltpu.make_async_copy(b_far, b_ref, sems.at[1]),
    ]
    for copy in copies:
        copy.start()
    for copy in copies:
        copy.wait()
    for i in range(BLOCKS):
        shift[i * LANES : (i + 1) * LANES, :] = upright(pot_ref[i : i + 1, :])

    @pl.loop(0, BLOCKS)
    def _(j):
        b = b_ref[pl.ds(pl.multiple_of(j * LANES, LANES), LANES), :]
        scores[...] = _dot(a_ref[...], b, NT) + shift[...]
        peak = jnp.max(scores[...], axis=0, keepdims=True)
        total = jnp.sum(jnp.exp(scores[...] - peak), axis=0, keepdims=True)
        for k in range(out_ref.shape[0]):
            out_ref[k, pl.ds(j, 1), :] = peak + jnp.log(total)


def first_kernel(
    me_ref, affinity_ref, firm_ref, *rest
):
    shares, rest = rest[:-7], rest[-7:]
    out_ref, means_ref, projected_ref, rows_ref, kept_ref, peaks_ref, scores = rest
    for k, part in enumerate(shares):
        rows = part.shape[0]
        begin = pl.multiple_of(jnp.bitwise_xor(me_ref[0], k) * rows, rows)
        means_ref[pl.ds(begin, rows), :] = part[...]
    projected_ref[...] = _dot(means_ref[...].astype(BF16), affinity_ref[...]).astype(BF16)
    rows_ref[...] = firm_ref[...].astype(BF16)
    for j in range(TILE // WIDE):
        slot = scores.at[j % 2]
        columns = slice(j * WIDE, (j + 1) * WIDE)
        b = projected_ref[columns, :]
        peak = None
        for t in range(TILE // WIDE):
            part = slice(t * WIDE, (t + 1) * WIDE)
            s = _dot(rows_ref[part, :], b, NT)
            slot[part, :] = s
            top = jnp.max(s.reshape(WIDE // 8, 8, WIDE), axis=0)
            peak = top if peak is None else jnp.maximum(peak, top)
        peak = jnp.max(peak, axis=0, keepdims=True)
        total = None
        for t in range(TILE // WIDE):
            part = slice(t * WIDE, (t + 1) * WIDE)
            e = jnp.exp(slot[part, :] - peak)
            kept_ref[part, columns] = e
            e = jnp.sum(e.reshape(WIDE // 8, 8, WIDE), axis=0)
            total = e if total is None else total + e
        lse = peak + jnp.log(jnp.sum(total, axis=0, keepdims=True))
        for i in range(WIDE // LANES):
            line = j * (WIDE // LANES) + i
            peaks_ref[line : line + 1, :] = peak[:, i * LANES : (i + 1) * LANES]
            spread_line(out_ref, line, lse[:, i * LANES : (i + 1) * LANES])


def column_kernel(
    mass, recv_ref, tally_ref, peaks_ref, kept_ref, a_ref, b_ref, out_ref, pot_ref, totals, *spare
):
    pot_ref[...] = combine(recv_ref, tally_ref, mass)
    level = peaks_ref[...] + pot_ref[...]
    top = jnp.max(level, keepdims=True)
    weight = jnp.exp(level - top)
    weights = [weight[t : t + 1, :] for t in range(BLOCKS)]
    for i in range(BLOCKS):
        rows = slice(i * LANES, (i + 1) * LANES)
        total = kept_ref[rows, 0:LANES] * weights[0]
        for t in range(1, BLOCKS):
            total += kept_ref[rows, t * LANES : (t + 1) * LANES] * weights[t]
        totals[i : i + 1, :] = jnp.sum(jnp.transpose(total), axis=0, keepdims=True)
    lse = top + jnp.log(totals[...])
    for k in range(out_ref.shape[0]):
        out_ref[k] = lse

    @pl.when(jnp.min(totals[...]) < TINY)
    def _():
        exact_lse(a_ref, b_ref, pot_ref, *spare, out_ref)


def row_kernel(
    mass, recv_ref, tally_ref, peaks_ref, kept_ref, a_ref, b_ref, out_ref, pot_ref, totals, *spare
):
    pot_ref[...] = combine(recv_ref, tally_ref, mass)
    top = jnp.max(pot_ref[...], keepdims=True)
    weight = jnp.exp(pot_ref[...] - top)
    total = [jnp.zeros((8, LANES), F32)] * BLOCKS
    for i in range(BLOCKS):
        rows = slice(i * LANES, (i + 1) * LANES)
        column = upright(weight[i : i + 1, :])
        for t in range(BLOCKS):
            e = kept_ref[rows, t * LANES : (t + 1) * LANES] * column
            total[t] = total[t] + jnp.sum(e.reshape(LANES // 8, 8, LANES), axis=0)
    for t in range(BLOCKS):
        totals[t : t + 1, :] = jnp.sum(total[t], axis=0, keepdims=True)
    lse = peaks_ref[...] + (top + jnp.log(totals[...]))
    for k in range(out_ref.shape[0]):
        out_ref[k] = lse

    @pl.when(jnp.min(totals[...]) < TINY)
    def _():
        exact_lse(a_ref, b_ref, pot_ref, *spare, out_ref)


def first_pass(me, affinity, firm_means, shares):
    wide = jax.ShapeDtypeStruct((TILE, K), BF16)
    return pl.pallas_call(
        first_kernel,
        out_shape=(
            jax.ShapeDtypeStruct((len(shares), BLOCKS, LANES), F32),
            jax.ShapeDtypeStruct((TILE, K), F32),
            wide,
            wide,
            pltpu.VMEM((TILE, TILE), F32),
            jax.ShapeDtypeStruct((BLOCKS, LANES), F32),
        ),
        in_specs=[SM] + [VM] * (2 + len(shares)),
        out_specs=(VM,) * 6,
        scratch_shapes=[pltpu.VMEM((2, TILE, WIDE), F32)],
        compiler_params=_params(40),
        cost_estimate=LIGHT,
        name="first_pass",
    )(me, affinity, firm_means, *shares)


def half_sweep(kernel, mass, recv, tally, peaks, kept, a, b, parts):
    small = jax.ShapeDtypeStruct((BLOCKS, LANES), F32)
    return pl.pallas_call(
        functools.partial(kernel, mass),
        out_shape=(jax.ShapeDtypeStruct((parts, BLOCKS, LANES), F32), small),
        in_specs=[VM] * 4 + [ANY] * 2,
        out_specs=(VM, VM),
        scratch_shapes=[
            pltpu.VMEM((BLOCKS, LANES), F32),
            pltpu.VMEM((TILE, LANES), F32),
            pltpu.VMEM((TILE, LANES), F32),
            pltpu.VMEM((TILE, K), BF16),
            pltpu.VMEM((TILE, K), BF16),
            pltpu.SemaphoreType.DMA((2,)),
        ],
        compiler_params=_params(24),
        cost_estimate=LIGHT,
        name=kernel.__name__,
    )(recv, tally, peaks, kept, a, b)


def last_kernel(mass, recv_ref, tally_ref, pot_ref):
    pot_ref[...] = combine(recv_ref, tally_ref, mass)


def last_pass(mass, recv, tally):
    return pl.pallas_call(
        functools.partial(last_kernel, mass),
        out_shape=jax.ShapeDtypeStruct((BLOCKS, LANES), F32),
        in_specs=[VM] * 2,
        out_specs=VM,
        compiler_params=_params(16),
        name="last_combine",
    )(recv, tally)


def swap(x, axis):
    return lax.all_to_all(x, axis, split_axis=0, concat_axis=0, tiled=True)


def pairs(parts, axis):
    count = lax.axis_size(axis)
    return [parts[0]] + [
        lax.ppermute(parts[s], axis, [(i, i ^ s) for i in range(count)]) for s in range(1, count)
    ]


def body(worker_ids, worker_attrs, firm_ids, firm_attrs, affinity):
    wa_count = lax.axis_size("wa")
    af_count = lax.axis_size("af")
    records_all = worker_ids.shape[0] * wa_count * af_count
    wa_me = lax.axis_index("wa").astype(jnp.int32).reshape(1)
    af_me = lax.axis_index("af").astype(jnp.int32).reshape(1)

    worker_sent = pack(worker_ids, worker_attrs, wa_count, None, affinity)
    worker_recv = swap(worker_sent[0], "wa")
    firm_sent = pack(firm_ids, firm_attrs, af_count, af_me, worker_sent[0])
    firm_recv = pairs(firm_sent, "af")
    worker_pooled = pool([worker_recv], af_count, None, firm_sent[0], LIGHT)
    worker_part = swap(worker_pooled[0], "af")
    firm_pooled = pool(firm_recv, wa_count, None, worker_pooled[0], HEAVY)
    firm_part = swap(firm_pooled[0], "wa")
    worker_mean, worker_tally = mean_share([worker_part], af_me, False, firm_pooled)
    worker_shares = pairs([worker_mean] * af_count, "af")
    firm_mean, firm_tally = mean_share([firm_part], wa_me, True, worker_shares[1:])
    firm_means = swap(firm_mean, "wa").reshape(TILE, K)

    partial, worker_means, projected, firm_rows, kept, peaks = first_pass(
        af_me, affinity, firm_means, worker_shares
    )
    for rounds in range(ITERS):
        partial, worker_potential = half_sweep(
            column_kernel,
            float(records_all + W),
            swap(partial, "af"),
            worker_tally,
            peaks,
            kept,
            projected,
            firm_rows,
            wa_count,
        )
        partial = swap(partial, "wa")
        if rounds < ITERS - 1:
            partial, unused = half_sweep(
                row_kernel,
                float(records_all + F),
                partial,
                firm_tally,
                peaks,
                kept,
                firm_rows,
                projected,
                af_count,
            )
    firm_potential = last_pass(float(records_all + F), partial, firm_tally)
    return (worker_means, firm_means, worker_potential.reshape(TILE), firm_potential.reshape(TILE))


def solution(mesh):
    placed = (P(("wa", "af")), P(("wa", "af"), None), P(("wa", "af")), P(("wa", "af"), None), P())
    return jax.shard_map(
        body,
        mesh=mesh,
        in_specs=placed,
        out_specs=(P("wa", None), P("af", None), P("wa"), P("af")),
        check_vma=False,
    )
```

```python
import functools
import math

import jax
import jax.numpy as jnp
from jax import lax
from jax.experimental import pallas as pl
from jax.experimental.pallas import tpu as pltpu
from jax.sharding import PartitionSpec as P

W = 32768
F = 16384
K = 128
ITERS = 3
TILE = 2048
LANES = 128
BLOCKS = TILE // LANES
ID_ROWS = 16
CHUNK = 512
WIDE = 256
TINY = 1e-25
F32 = jnp.float32
BF16 = jnp.bfloat16

VM = pl.BlockSpec(memory_space=pltpu.VMEM)
SM = pl.BlockSpec(memory_space=pltpu.SMEM)
FAR = pl.BlockSpec(memory_space=pltpu.HBM)
LIGHT = pl.CostEstimate(flops=1 << 20, bytes_accessed=1 << 16, transcendentals=0)
NT = (((1,), (1,)), ((), ()))
NN = (((1,), (0,)), ((), ()))


def _far(x):
    return pltpu.with_memory_space_constraint(x, pltpu.HBM)


def _params(mib):
    return pltpu.CompilerParams(vmem_limit_bytes=mib << 20)


def _dot(a, b, dims=NN):
    return lax.dot_general(a, b, dims, preferred_element_type=F32)


def _flag(mask):
    return jnp.where(mask, 1.0, 0.0).astype(BF16)


def pack_kernel(groups, capacity, me_ref, ids_ref, attrs_ref, after_ref, *rest):
    outs, (dest_v, dest_s, near, wide, placed, sems) = rest[:-6], rest[-6:]
    fetch = pltpu.make_async_copy(attrs_ref, near, sems.at[0])
    fetch.start()
    rows = ids_ref.shape[0]
    ids = ids_ref[...]
    owner = jnp.bitwise_xor(lax.shift_right_logical(ids, 11), me_ref[0])
    local = jnp.bitwise_and(ids, TILE - 1)
    sub = lax.broadcasted_iota(jnp.int32, (LANES, LANES), 0)
    lane = lax.broadcasted_iota(jnp.int32, (LANES, LANES), 1)
    before = _flag(sub < lane)
    every = jnp.ones((LANES, LANES), BF16)
    above = _flag(
        lax.broadcasted_iota(jnp.int32, (rows, rows), 1)
        < lax.broadcasted_iota(jnp.int32, (rows, rows), 0)
    )
    masks = [owner == g for g in range(groups)]
    stacked = jnp.concatenate([_flag(m) for m in masks], axis=0)
    inside = _dot(stacked, before)
    totals = _dot(stacked, every).astype(BF16)
    slot = jnp.zeros((rows, LANES), F32)
    for g in range(groups):
        part = slice(g * rows, (g + 1) * rows)
        slot = jnp.where(masks[g], inside[part] + _dot(above, totals[part]), slot)
    slot = slot.astype(jnp.int32)
    dest_v[...] = owner * capacity + slot
    to_scalar = pltpu.make_async_copy(dest_v, dest_s, sems.at[1])
    to_scalar.start()

    line = lax.shift_right_logical(slot, 7)
    column = jnp.bitwise_and(slot, LANES - 1)
    high_row = owner * ID_ROWS + line
    low_row = high_row + capacity // LANES
    high = (lax.shift_right_logical(local, 6) + 1).astype(F32)
    low = jnp.bitwise_and(local, 63).astype(F32)
    place = lax.broadcasted_iota(jnp.int32, (groups * ID_ROWS, LANES), 0)
    packed = jnp.zeros((groups * ID_ROWS, LANES), F32)
    for c in range(rows):
        r = slice(c, c + 1)
        values = jnp.where(place == high_row[r], high[r], 0.0) + jnp.where(
            place == low_row[r], low[r], 0.0
        )
        packed += _dot(values.astype(BF16), _flag(sub == column[r]), NT)
    packed = packed.astype(BF16)
    for g in range(groups):
        behind = packed[g * ID_ROWS : (g + 1) * ID_ROWS]
        if len(outs) == 1:
            outs[0][g, capacity : capacity + ID_ROWS, :] = behind
        else:
            outs[g][capacity : capacity + ID_ROWS, :] = behind

    placed[...] = jnp.zeros_like(placed)
    fetch.wait()
    wide[...] = near[...].astype(F32)
    to_scalar.wait()

    @pl.loop(0, rows)
    def _(row):
        first = pl.multiple_of(row * LANES, LANES)
        held = [wide[pl.ds(first + u, 1), :] for u in range(LANES)]
        to = [dest_s[row, u] for u in range(LANES)]
        for u in range(LANES):
            placed[pl.ds(to[u], 1), :] = held[u]

    for g in range(groups):
        group = placed[g * capacity : (g + 1) * capacity, :].astype(BF16)
        if len(outs) == 1:
            outs[0][g, 0:capacity, :] = group
        else:
            outs[g][0:capacity, :] = group


def pack(ids, attrs, groups, me, after):
    rows = ids.shape[0]
    capacity = 2 * rows // groups
    if me is None:
        me = jnp.zeros((1,), jnp.int32)
        made = (jax.ShapeDtypeStruct((groups, capacity + ID_ROWS, K), BF16),)
    else:
        made = (jax.ShapeDtypeStruct((capacity + ID_ROWS, K), BF16),) * groups
    return pl.pallas_call(
        functools.partial(pack_kernel, groups, capacity),
        out_shape=made,
        in_specs=[SM, VM, FAR, FAR],
        out_specs=(VM,) * len(made),
        scratch_shapes=[
            pltpu.VMEM((rows // LANES, LANES), jnp.int32),
            pltpu.SMEM((rows // LANES, LANES), jnp.int32),
            pltpu.VMEM((rows, K), BF16),
            pltpu.VMEM((rows, K), F32),
            pltpu.VMEM((groups * capacity, K), F32),
            pltpu.SemaphoreType.DMA((2,)),
        ],
        compiler_params=_params(24),
        cost_estimate=LIGHT,
        name="pack_records",
    )(me, ids.reshape(rows // LANES, LANES), _far(attrs), _far(after))


def pool_kernel(groups, capacity, split, behind, me_ref, *rest):
    recvs, outs, rest = rest[behind : -split - 3], rest[-split - 3 : -3], rest[-3:]
    sums, tallies, more = rest
    if len(recvs) == 1:
        recvs = [recvs[0].at[g] for g in range(groups)]
    half = capacity // 2
    lines = capacity // LANES
    types = lax.broadcasted_iota(jnp.int32, (TILE // 2, CHUNK), 0)

    def ids_of(recv, begin, end):
        coded = recv[capacity : capacity + ID_ROWS, :].astype(F32).astype(jnp.int32)
        return [
            (coded[i : i + 1] - 1) * 64 + coded[lines + i : lines + i + 1]
            for i in range(begin, end)
        ]

    def add(ids, x, fresh=False):
        upper = [
            jnp.where(upright(i.astype(F32)) >= TILE // 2, 1.0, 0.0).astype(BF16) for i in ids
        ]
        high = x * jnp.concatenate(upper, axis=0)
        both = jnp.concatenate([x - high, high], axis=1)
        ids = jnp.concatenate(ids, axis=1)
        wide = ids.shape[1]
        folded = jnp.where(ids >= TILE // 2, ids - TILE // 2, ids)
        total = _dot(_flag(types[:, :wide] == folded), both)
        line = jnp.right_shift(ids, 7)
        column = jnp.bitwise_and(ids, LANES - 1)
        tally = _dot(
            _flag(types[:BLOCKS, :wide] == line), _flag(types[:LANES, :wide] == column), NT
        )
        for side in range(2):
            part = total[:, side * K : (side + 1) * K]
            sums[side] = part if fresh else sums[side] + part
        tallies[...] = tally if fresh else tallies[...] + tally

    for g in range(groups):
        more[g] = jnp.max(
            recvs[g][capacity : capacity + ID_ROWS, :].astype(F32)[lines // 2 : lines]
        ).astype(jnp.int32)
    together = max(1, CHUNK // half)
    for g in range(0, groups, together):
        ids = [i for k in range(together) for i in ids_of(recvs[g + k], 0, lines // 2)]
        x = [recvs[g + k][0:half, :] for k in range(together)]
        add(ids, x[0] if together == 1 else jnp.concatenate(x, axis=0), g == 0)
    for g in range(groups):

        @pl.when(more[g] > 0)
        def _(recv=recvs[g]):
            add(ids_of(recv, lines // 2, lines), recv[half:capacity, :])

    if split == 1:
        parts = outs[0].shape[0]
        share = TILE // parts
        for k in range(parts):
            side, row = divmod(k * share, TILE // 2)
            outs[0][k, 0:share, :] = sums[side, row : row + share, :]
            outs[0][k, share : share + BLOCKS, :] = tallies[...]
        return
    parts = outs[0].shape[0]
    share = TILE // (parts * split)
    for c in range(split):
        for k in range(parts):
            begin = jnp.bitwise_xor(me_ref[0], split * k + c) * share
            side = begin // (TILE // 2)
            row = pl.multiple_of(begin - side * (TILE // 2), share)
            outs[c][k, 0:share, :] = sums[side, pl.ds(row, share), :]
            outs[c][k, share : share + BLOCKS, :] = tallies[...]


def pool(recvs, parts, me, after):
    if len(recvs) == 1:
        groups, depth = recvs[0].shape[:2]
    else:
        groups, depth = len(recvs), recvs[0].shape[0]
    rows = TILE // parts + BLOCKS
    if me is None:
        me = jnp.zeros((1,), jnp.int32)
        made = (jax.ShapeDtypeStruct((parts, rows, K), F32),)
    else:
        made = (jax.ShapeDtypeStruct((parts // 2, rows, K), F32),) * 2
    return pl.pallas_call(
        functools.partial(pool_kernel, groups, depth - ID_ROWS, len(made), len(after)),
        out_shape=made,
        in_specs=[SM] + [FAR] * len(after) + [VM] * len(recvs),
        out_specs=(VM,) * len(made),
        scratch_shapes=[
            pltpu.VMEM((2, TILE // 2, K), F32),
            pltpu.VMEM((BLOCKS, LANES), F32),
            pltpu.SMEM((groups,), jnp.int32),
        ],
        compiler_params=_params(24),
        cost_estimate=LIGHT,
        name="pool_records",
    )(me, *[_far(x) for x in after], *recvs)


def merge_kernel(mine_ref, other_ref, *outs):
    for k, out in enumerate(outs):
        out[...] = mine_ref[k] + other_ref[k]


def merge(mine, other):
    parts, rows, width = mine.shape
    return pl.pallas_call(
        merge_kernel,
        out_shape=(jax.ShapeDtypeStruct((rows, width), F32),) * parts,
        in_specs=[VM, VM],
        out_specs=(VM,) * parts,
        compiler_params=_params(24),
        cost_estimate=LIGHT,
        name="merge_cores",
    )(mine, other)


def upright(row):
    return jnp.transpose(jnp.broadcast_to(row, (LANES, LANES)))


def mean_kernel(share, spread, behind, me_ref, *rest):
    recvs, (mean_ref, tally_ref) = rest[behind:-2], rest[-2:]
    if len(recvs) == 1:
        recvs = [recvs[0].at[k] for k in range(recvs[0].shape[0])]
    tally = recvs[0][share : share + BLOCKS, :]
    total = recvs[0][0:share, :]
    for recv in recvs[1:]:
        tally += recv[share : share + BLOCKS, :]
        total += recv[0:share, :]
    tally_ref[...] = tally
    me = me_ref[0]
    lines = share // LANES
    counts = jnp.concatenate(
        [upright(tally_ref[pl.ds(me * lines + i, 1), :]) for i in range(lines)], axis=0
    )
    means = total / jnp.maximum(counts, 1.0)
    if spread:
        for k in range(len(recvs)):
            mean_ref[k] = means
    else:
        mean_ref[...] = means


def mean_share(recvs, me, spread, after):
    parts = recvs[0].shape[0] if len(recvs) == 1 else len(recvs)
    share = recvs[0].shape[-2] - BLOCKS
    made = jax.ShapeDtypeStruct((parts, share, K) if spread else (share, K), F32)
    return pl.pallas_call(
        functools.partial(mean_kernel, share, spread, len(after)),
        out_shape=(made, jax.ShapeDtypeStruct((BLOCKS, LANES), F32)),
        in_specs=[SM] + [FAR] * len(after) + [VM] * len(recvs),
        out_specs=(VM,) * 2,
        compiler_params=_params(24),
        cost_estimate=LIGHT,
        name="mean_share",
    )(me, *[_far(x) for x in after], *recvs)


def combine(recv_ref, tally_ref, mass):
    peak = recv_ref[0]
    for k in range(1, recv_ref.shape[0]):
        peak = jnp.maximum(peak, recv_ref[k])
    total = jnp.exp(recv_ref[0] - peak)
    for k in range(1, recv_ref.shape[0]):
        total += jnp.exp(recv_ref[k] - peak)
    return (jnp.log(tally_ref[...] + 1.0) - math.log(mass)) - (peak + jnp.log(total))


def spread_line(out_ref, line, row):
    for k in range(out_ref.shape[0]):
        out_ref[k, line : line + 1, :] = row


def exact_lse(a_far, b_far, pot_ref, shift, scores, a_ref, b_ref, sems, out_ref):
    copies = [
        pltpu.make_async_copy(a_far, a_ref, sems.at[0]),
        pltpu.make_async_copy(b_far, b_ref, sems.at[1]),
    ]
    for copy in copies:
        copy.start()
    for copy in copies:
        copy.wait()
    for i in range(BLOCKS):
        shift[i * LANES : (i + 1) * LANES, :] = upright(pot_ref[i : i + 1, :])

    @pl.loop(0, BLOCKS)
    def _(j):
        b = b_ref[pl.ds(pl.multiple_of(j * LANES, LANES), LANES), :]
        scores[...] = _dot(a_ref[...], b, NT) + shift[...]
        peak = jnp.max(scores[...], axis=0, keepdims=True)
        total = jnp.sum(jnp.exp(scores[...] - peak), axis=0, keepdims=True)
        for k in range(out_ref.shape[0]):
            out_ref[k, pl.ds(j, 1), :] = peak + jnp.log(total)


def first_kernel(
    me_ref, affinity_ref, firm_ref, *rest
):
    shares, rest = rest[:-8], rest[-8:]
    out_ref, means_ref, projected_ref, rows_ref, kept_ref, peaks_ref, firm_out_ref, scores = rest
    firm_out_ref[...] = firm_ref[...]
    rows_ref[...] = firm_ref[...].astype(BF16)
    for k, part in enumerate(shares):
        rows = part.shape[0]
        begin = pl.multiple_of(jnp.bitwise_xor(me_ref[0], k) * rows, rows)
        means_ref[pl.ds(begin, rows), :] = part[...]
    projected_ref[...] = _dot(means_ref[...].astype(BF16), affinity_ref[...]).astype(BF16)
    for j in range(TILE // WIDE):
        slot = scores.at[j % 2]
        columns = slice(j * WIDE, (j + 1) * WIDE)
        b = projected_ref[columns, :]
        peak = None
        for t in range(TILE // WIDE):
            part = slice(t * WIDE, (t + 1) * WIDE)
            s = _dot(rows_ref[part, :], b, NT)
            slot[part, :] = s
            top = jnp.max(s.reshape(WIDE // 8, 8, WIDE), axis=0)
            peak = top if peak is None else jnp.maximum(peak, top)
        peak = jnp.max(peak, axis=0, keepdims=True)
        total = None
        for t in range(TILE // WIDE):
            part = slice(t * WIDE, (t + 1) * WIDE)
            e = jnp.exp(slot[part, :] - peak)
            kept_ref[part, columns] = e
            e = jnp.sum(e.reshape(WIDE // 8, 8, WIDE), axis=0)
            total = e if total is None else total + e
        lse = peak + jnp.log(jnp.sum(total, axis=0, keepdims=True))
        for i in range(WIDE // LANES):
            line = j * (WIDE // LANES) + i
            peaks_ref[line : line + 1, :] = peak[:, i * LANES : (i + 1) * LANES]
            spread_line(out_ref, line, lse[:, i * LANES : (i + 1) * LANES])


def column_kernel(
    mass, recv_ref, tally_ref, peaks_ref, kept_ref, a_ref, b_ref, out_ref, pot_ref, totals, *spare
):
    pot_ref[...] = combine(recv_ref, tally_ref, mass)
    level = peaks_ref[...] + pot_ref[...]
    top = jnp.max(level, keepdims=True)
    weight = jnp.exp(level - top)
    weights = [weight[t : t + 1, :] for t in range(BLOCKS)]
    for i in range(BLOCKS):
        rows = slice(i * LANES, (i + 1) * LANES)
        total = kept_ref[rows, 0:LANES] * weights[0]
        for t in range(1, BLOCKS):
            total += kept_ref[rows, t * LANES : (t + 1) * LANES] * weights[t]
        totals[i : i + 1, :] = jnp.sum(jnp.transpose(total), axis=0, keepdims=True)
    lse = top + jnp.log(totals[...])
    for k in range(out_ref.shape[0]):
        out_ref[k] = lse

    @pl.when(jnp.min(totals[...]) < TINY)
    def _():
        exact_lse(a_ref, b_ref, pot_ref, *spare, out_ref)


def row_kernel(
    mass, recv_ref, tally_ref, peaks_ref, kept_ref, a_ref, b_ref, out_ref, pot_ref, totals, *spare
):
    pot_ref[...] = combine(recv_ref, tally_ref, mass)
    top = jnp.max(pot_ref[...], keepdims=True)
    weight = jnp.exp(pot_ref[...] - top)
    total = [jnp.zeros((8, LANES), F32)] * BLOCKS
    for i in range(BLOCKS):
        rows = slice(i * LANES, (i + 1) * LANES)
        column = upright(weight[i : i + 1, :])
        for t in range(BLOCKS):
            e = kept_ref[rows, t * LANES : (t + 1) * LANES] * column
            total[t] = total[t] + jnp.sum(e.reshape(LANES // 8, 8, LANES), axis=0)
    for t in range(BLOCKS):
        totals[t : t + 1, :] = jnp.sum(total[t], axis=0, keepdims=True)
    lse = peaks_ref[...] + (top + jnp.log(totals[...]))
    for k in range(out_ref.shape[0]):
        out_ref[k] = lse

    @pl.when(jnp.min(totals[...]) < TINY)
    def _():
        exact_lse(a_ref, b_ref, pot_ref, *spare, out_ref)


def first_pass(me, affinity, firm_rows, shares):
    return pl.pallas_call(
        first_kernel,
        out_shape=(
            jax.ShapeDtypeStruct((len(shares), BLOCKS, LANES), F32),
            jax.ShapeDtypeStruct((TILE, K), F32),
            jax.ShapeDtypeStruct((TILE, K), BF16),
            jax.ShapeDtypeStruct((TILE, K), BF16),
            pltpu.VMEM((TILE, TILE), F32),
            jax.ShapeDtypeStruct((BLOCKS, LANES), F32),
            jax.ShapeDtypeStruct((TILE, K), F32),
        ),
        in_specs=[SM] + [VM] * (2 + len(shares)),
        out_specs=(VM,) * 7,
        scratch_shapes=[pltpu.VMEM((2, TILE, WIDE), F32)],
        compiler_params=_params(40),
        cost_estimate=LIGHT,
        name="first_pass",
    )(me, affinity, firm_rows, *shares)


def half_sweep(kernel, mass, recv, tally, peaks, kept, a, b, parts):
    small = jax.ShapeDtypeStruct((BLOCKS, LANES), F32)
    return pl.pallas_call(
        functools.partial(kernel, mass),
        out_shape=(jax.ShapeDtypeStruct((parts, BLOCKS, LANES), F32), small),
        in_specs=[VM] * 4 + [FAR] * 2,
        out_specs=(VM, VM),
        scratch_shapes=[
            pltpu.VMEM((BLOCKS, LANES), F32),
            pltpu.VMEM((TILE, LANES), F32),
            pltpu.VMEM((TILE, LANES), F32),
            pltpu.VMEM((TILE, K), BF16),
            pltpu.VMEM((TILE, K), BF16),
            pltpu.SemaphoreType.DMA((2,)),
        ],
        compiler_params=_params(24),
        cost_estimate=LIGHT,
        name=kernel.__name__,
    )(recv, tally, peaks, kept, _far(a), _far(b))


def last_kernel(mass, recv_ref, tally_ref, pot_ref):
    pot_ref[...] = combine(recv_ref, tally_ref, mass)


def last_pass(mass, recv, tally):
    return pl.pallas_call(
        functools.partial(last_kernel, mass),
        out_shape=jax.ShapeDtypeStruct((BLOCKS, LANES), F32),
        in_specs=[VM] * 2,
        out_specs=VM,
        compiler_params=_params(16),
        cost_estimate=LIGHT,
        name="last_combine",
    )(recv, tally)


def swap(x, axis):
    return lax.all_to_all(x, axis, split_axis=0, concat_axis=0, tiled=True)


def trade(x, axis, s):
    return lax.ppermute(x, axis, [(i, i ^ s) for i in range(lax.axis_size(axis))])


def pairs(parts, axis, step=1):
    return [parts[0]] + [trade(parts[k], axis, step * k) for k in range(1, len(parts))]


def body(worker_ids, worker_attrs, firm_ids, firm_attrs, affinity):
    wa_count = lax.axis_size("wa")
    af_count = lax.axis_size("af")
    records_all = worker_ids.shape[0] * wa_count * af_count
    wa_me = lax.axis_index("wa").astype(jnp.int32).reshape(1)
    af_me = lax.axis_index("af").astype(jnp.int32).reshape(1)

    worker_sent = pack(worker_ids, worker_attrs, wa_count, None, affinity)
    worker_recv = swap(worker_sent[0], "wa")
    firm_sent = pack(firm_ids, firm_attrs, af_count, af_me, worker_sent[0])
    firm_recv = pairs(firm_sent, "af")
    firm_pooled = pool(firm_recv, wa_count, None, [worker_sent[0]])
    firm_part = swap(firm_pooled[0], "wa")
    worker_pooled = pool([worker_recv], af_count, af_me, firm_pooled)
    worker_chip = merge(worker_pooled[0], trade(worker_pooled[1], "af", 1))
    worker_part = pairs(worker_chip, "af", 2)
    firm_mean, firm_tally = mean_share([firm_part], wa_me, True, worker_part[1:])
    firm_means = swap(firm_mean, "wa").reshape(TILE, K)
    worker_mean, worker_tally = mean_share(worker_part, af_me, False, [firm_mean])
    worker_shares = pairs([worker_mean] * af_count, "af")

    partial, worker_means, projected, firm_rows, kept, peaks, firm_means = first_pass(
        af_me, affinity, firm_means, worker_shares
    )
    for rounds in range(ITERS):
        partial, worker_potential = half_sweep(
            column_kernel,
            float(records_all + W),
            swap(partial, "af"),
            worker_tally,
            peaks,
            kept,
            projected,
            firm_rows,
            wa_count,
        )
        partial = swap(partial, "wa")
        if rounds < ITERS - 1:
            partial, unused = half_sweep(
                row_kernel,
                float(records_all + F),
                partial,
                firm_tally,
                peaks,
                kept,
                firm_rows,
                projected,
                af_count,
            )
    firm_potential = last_pass(float(records_all + F), partial, firm_tally)
    return (worker_means, firm_means, worker_potential.reshape(TILE), firm_potential.reshape(TILE))


def solution(mesh):
    placed = (P(("wa", "af")), P(("wa", "af"), None), P(("wa", "af")), P(("wa", "af"), None), P())
    return jax.shard_map(
        body,
        mesh=mesh,
        in_specs=placed,
        out_specs=(P("wa", None), P("af", None), P("wa"), P("af")),
        check_vma=False,
    )
```

```python
import functools
import math

import jax
import jax.numpy as jnp
from jax import lax
from jax.experimental import pallas as pl
from jax.experimental.pallas import tpu as pltpu
from jax.sharding import PartitionSpec as P

W = 32768
F = 16384
K = 128
ITERS = 3
TILE = 2048
LANES = 128
BLOCKS = TILE // LANES
ID_ROWS = 16
CHUNK = 512
WIDE = 256
TINY = 1e-25
F32 = jnp.float32
BF16 = jnp.bfloat16

VM = pl.BlockSpec(memory_space=pltpu.VMEM)
SM = pl.BlockSpec(memory_space=pltpu.SMEM)
FAR = pl.BlockSpec(memory_space=pltpu.HBM)
LIGHT = pl.CostEstimate(flops=1 << 20, bytes_accessed=1 << 16, transcendentals=0)
NT = (((1,), (1,)), ((), ()))
NN = (((1,), (0,)), ((), ()))


def _far(x):
    return pltpu.with_memory_space_constraint(x, pltpu.HBM)


def _params(mib):
    return pltpu.CompilerParams(vmem_limit_bytes=mib << 20)


def _dot(a, b, dims=NN):
    return lax.dot_general(a, b, dims, preferred_element_type=F32)


def _flag(mask):
    return jnp.where(mask, 1.0, 0.0).astype(BF16)


def pack_kernel(groups, capacity, me_ref, ids_ref, attrs_ref, after_ref, *rest):
    outs, (dest_v, dest_s, near, wide, placed, sems) = rest[:-6], rest[-6:]
    fetch = pltpu.make_async_copy(attrs_ref, near, sems.at[0])
    fetch.start()
    rows = ids_ref.shape[0]
    ids = ids_ref[...]
    owner = jnp.bitwise_xor(lax.shift_right_logical(ids, 11), me_ref[0])
    local = jnp.bitwise_and(ids, TILE - 1)
    sub = lax.broadcasted_iota(jnp.int32, (LANES, LANES), 0)
    lane = lax.broadcasted_iota(jnp.int32, (LANES, LANES), 1)
    before = _flag(sub < lane)
    every = jnp.ones((LANES, LANES), BF16)
    above = _flag(
        lax.broadcasted_iota(jnp.int32, (rows, rows), 1)
        < lax.broadcasted_iota(jnp.int32, (rows, rows), 0)
    )
    masks = [owner == g for g in range(groups)]
    stacked = jnp.concatenate([_flag(m) for m in masks], axis=0)
    inside = _dot(stacked, before)
    totals = _dot(stacked, every).astype(BF16)
    slot = jnp.zeros((rows, LANES), F32)
    for g in range(groups):
        part = slice(g * rows, (g + 1) * rows)
        slot = jnp.where(masks[g], inside[part] + _dot(above, totals[part]), slot)
    slot = slot.astype(jnp.int32)
    dest_v[...] = owner * capacity + slot
    to_scalar = pltpu.make_async_copy(dest_v, dest_s, sems.at[1])
    to_scalar.start()

    line = lax.shift_right_logical(slot, 7)
    column = jnp.bitwise_and(slot, LANES - 1)
    high_row = owner * ID_ROWS + line
    low_row = high_row + capacity // LANES
    high = (lax.shift_right_logical(local, 6) + 1).astype(F32)
    low = jnp.bitwise_and(local, 63).astype(F32)
    place = lax.broadcasted_iota(jnp.int32, (groups * ID_ROWS, LANES), 0)
    packed = jnp.zeros((groups * ID_ROWS, LANES), F32)
    for c in range(rows):
        r = slice(c, c + 1)
        values = jnp.where(place == high_row[r], high[r], 0.0) + jnp.where(
            place == low_row[r], low[r], 0.0
        )
        packed += _dot(values.astype(BF16), _flag(sub == column[r]), NT)
    packed = packed.astype(BF16)
    for g in range(groups):
        behind = packed[g * ID_ROWS : (g + 1) * ID_ROWS]
        if len(outs) == 1:
            outs[0][g, capacity : capacity + ID_ROWS, :] = behind
        else:
            outs[g][capacity : capacity + ID_ROWS, :] = behind

    placed[...] = jnp.zeros_like(placed)
    fetch.wait()
    wide[...] = near[...].astype(F32)
    to_scalar.wait()

    @pl.loop(0, rows)
    def _(row):
        first = pl.multiple_of(row * LANES, LANES)
        held = [wide[pl.ds(first + u, 1), :] for u in range(LANES)]
        to = [dest_s[row, u] for u in range(LANES)]
        for u in range(LANES):
            placed[pl.ds(to[u], 1), :] = held[u]

    for g in range(groups):
        group = placed[g * capacity : (g + 1) * capacity, :].astype(BF16)
        if len(outs) == 1:
            outs[0][g, 0:capacity, :] = group
        else:
            outs[g][0:capacity, :] = group


def pack(ids, attrs, groups, me, after):
    rows = ids.shape[0]
    capacity = 2 * rows // groups
    if me is None:
        me = jnp.zeros((1,), jnp.int32)
        made = (jax.ShapeDtypeStruct((groups, capacity + ID_ROWS, K), BF16),)
    else:
        made = (jax.ShapeDtypeStruct((capacity + ID_ROWS, K), BF16),) * groups
    return pl.pallas_call(
        functools.partial(pack_kernel, groups, capacity),
        out_shape=made,
        in_specs=[SM, VM, FAR, FAR],
        out_specs=(VM,) * len(made),
        scratch_shapes=[
            pltpu.VMEM((rows // LANES, LANES), jnp.int32),
            pltpu.SMEM((rows // LANES, LANES), jnp.int32),
            pltpu.VMEM((rows, K), BF16),
            pltpu.VMEM((rows, K), F32),
            pltpu.VMEM((groups * capacity, K), F32),
            pltpu.SemaphoreType.DMA((2,)),
        ],
        compiler_params=_params(24),
        cost_estimate=LIGHT,
        name="pack_records",
    )(me, ids.reshape(rows // LANES, LANES), _far(attrs), _far(after))


def pool_kernel(groups, capacity, split, behind, me_ref, *rest):
    recvs, outs, rest = rest[behind : -split - 3], rest[-split - 3 : -3], rest[-3:]
    sums, tallies, more = rest
    if len(recvs) == 1:
        recvs = [recvs[0].at[g] for g in range(groups)]
    half = capacity // 2
    lines = capacity // LANES
    types = lax.broadcasted_iota(jnp.int32, (TILE // 2, CHUNK), 0)

    def ids_of(recv, begin, end):
        coded = recv[capacity : capacity + ID_ROWS, :].astype(F32).astype(jnp.int32)
        return [
            (coded[i : i + 1] - 1) * 64 + coded[lines + i : lines + i + 1]
            for i in range(begin, end)
        ]

    def add(ids, x, fresh=False):
        upper = [
            jnp.where(upright(i.astype(F32)) >= TILE // 2, 1.0, 0.0).astype(BF16) for i in ids
        ]
        high = x * jnp.concatenate(upper, axis=0)
        both = jnp.concatenate([x - high, high], axis=1)
        ids = jnp.concatenate(ids, axis=1)
        wide = ids.shape[1]
        folded = jnp.where(ids >= TILE // 2, ids - TILE // 2, ids)
        total = _dot(_flag(types[:, :wide] == folded), both)
        line = jnp.right_shift(ids, 7)
        column = jnp.bitwise_and(ids, LANES - 1)
        tally = _dot(
            _flag(types[:BLOCKS, :wide] == line), _flag(types[:LANES, :wide] == column), NT
        )
        for side in range(2):
            part = total[:, side * K : (side + 1) * K]
            sums[side] = part if fresh else sums[side] + part
        tallies[...] = tally if fresh else tallies[...] + tally

    for g in range(groups):
        more[g] = jnp.max(
            recvs[g][capacity : capacity + ID_ROWS, :].astype(F32)[lines // 2 : lines]
        ).astype(jnp.int32)
    together = max(1, CHUNK // half)
    for g in range(0, groups, together):
        ids = [i for k in range(together) for i in ids_of(recvs[g + k], 0, lines // 2)]
        x = [recvs[g + k][0:half, :] for k in range(together)]
        add(ids, x[0] if together == 1 else jnp.concatenate(x, axis=0), g == 0)
    for g in range(groups):

        @pl.when(more[g] > 0)
        def _(recv=recvs[g]):
            add(ids_of(recv, lines // 2, lines), recv[half:capacity, :])

    if split == 1:
        parts = outs[0].shape[0]
        share = TILE // parts
        for k in range(parts):
            side, row = divmod(k * share, TILE // 2)
            outs[0][k, 0:share, :] = sums[side, row : row + share, :]
            outs[0][k, share : share + BLOCKS, :] = tallies[...]
        return
    parts = outs[0].shape[0]
    share = TILE // (parts * split)
    for c in range(split):
        for k in range(parts):
            begin = jnp.bitwise_xor(me_ref[0], split * k + c) * share
            side = begin // (TILE // 2)
            row = pl.multiple_of(begin - side * (TILE // 2), share)
            outs[c][k, 0:share, :] = sums[side, pl.ds(row, share), :]
            outs[c][k, share : share + BLOCKS, :] = tallies[...]


def pool(recvs, parts, me, after):
    if len(recvs) == 1:
        groups, depth = recvs[0].shape[:2]
    else:
        groups, depth = len(recvs), recvs[0].shape[0]
    rows = TILE // parts + BLOCKS
    if me is None:
        me = jnp.zeros((1,), jnp.int32)
        made = (jax.ShapeDtypeStruct((parts, rows, K), F32),)
    else:
        made = (jax.ShapeDtypeStruct((parts // 2, rows, K), F32),) * 2
    return pl.pallas_call(
        functools.partial(pool_kernel, groups, depth - ID_ROWS, len(made), len(after)),
        out_shape=made,
        in_specs=[SM] + [FAR] * len(after) + [VM] * len(recvs),
        out_specs=(VM,) * len(made),
        scratch_shapes=[
            pltpu.VMEM((2, TILE // 2, K), F32),
            pltpu.VMEM((BLOCKS, LANES), F32),
            pltpu.SMEM((groups,), jnp.int32),
        ],
        compiler_params=_params(24),
        cost_estimate=LIGHT,
        name="pool_records",
    )(me, *[_far(x) for x in after], *recvs)


def merge_kernel(mine_ref, other_ref, *outs):
    for k, out in enumerate(outs):
        out[...] = mine_ref[k] + other_ref[k]


def merge(mine, other):
    parts, rows, width = mine.shape
    return pl.pallas_call(
        merge_kernel,
        out_shape=(jax.ShapeDtypeStruct((rows, width), F32),) * parts,
        in_specs=[VM, VM],
        out_specs=(VM,) * parts,
        compiler_params=_params(24),
        cost_estimate=LIGHT,
        name="merge_cores",
    )(mine, other)


def upright(row):
    return jnp.transpose(jnp.broadcast_to(row, (LANES, LANES)))


def mean_kernel(share, spread, behind, me_ref, *rest):
    recvs, (mean_ref, tally_ref) = rest[behind:-2], rest[-2:]
    if len(recvs) == 1:
        recvs = [recvs[0].at[k] for k in range(recvs[0].shape[0])]
    tally = recvs[0][share : share + BLOCKS, :]
    total = recvs[0][0:share, :]
    for recv in recvs[1:]:
        tally += recv[share : share + BLOCKS, :]
        total += recv[0:share, :]
    tally_ref[...] = tally
    me = me_ref[0]
    lines = share // LANES
    counts = jnp.concatenate(
        [upright(tally_ref[pl.ds(me * lines + i, 1), :]) for i in range(lines)], axis=0
    )
    means = total / jnp.maximum(counts, 1.0)
    if spread:
        for k in range(len(recvs)):
            mean_ref[k] = means
    else:
        mean_ref[...] = means


def mean_share(recvs, me, spread, after):
    parts = recvs[0].shape[0] if len(recvs) == 1 else len(recvs)
    share = recvs[0].shape[-2] - BLOCKS
    made = jax.ShapeDtypeStruct((parts, share, K) if spread else (share, K), F32)
    return pl.pallas_call(
        functools.partial(mean_kernel, share, spread, len(after)),
        out_shape=(made, jax.ShapeDtypeStruct((BLOCKS, LANES), F32)),
        in_specs=[SM] + [FAR] * len(after) + [VM] * len(recvs),
        out_specs=(VM,) * 2,
        compiler_params=_params(24),
        cost_estimate=LIGHT,
        name="mean_share",
    )(me, *[_far(x) for x in after], *recvs)


def combine(recv_ref, tally_ref, mass):
    peak = recv_ref[0]
    for k in range(1, recv_ref.shape[0]):
        peak = jnp.maximum(peak, recv_ref[k])
    total = jnp.exp(recv_ref[0] - peak)
    for k in range(1, recv_ref.shape[0]):
        total += jnp.exp(recv_ref[k] - peak)
    return (jnp.log(tally_ref[...] + 1.0) - math.log(mass)) - (peak + jnp.log(total))


def spread_line(out_ref, line, row):
    for k in range(out_ref.shape[0]):
        out_ref[k, line : line + 1, :] = row


def exact_lse(a_far, b_far, pot_ref, shift, scores, a_ref, b_ref, sems, out_ref):
    copies = [
        pltpu.make_async_copy(a_far, a_ref, sems.at[0]),
        pltpu.make_async_copy(b_far, b_ref, sems.at[1]),
    ]
    for copy in copies:
        copy.start()
    for copy in copies:
        copy.wait()
    for i in range(BLOCKS):
        shift[i * LANES : (i + 1) * LANES, :] = upright(pot_ref[i : i + 1, :])

    @pl.loop(0, BLOCKS)
    def _(j):
        b = b_ref[pl.ds(pl.multiple_of(j * LANES, LANES), LANES), :]
        scores[...] = _dot(a_ref[...], b, NT) + shift[...]
        peak = jnp.max(scores[...], axis=0, keepdims=True)
        total = jnp.sum(jnp.exp(scores[...] - peak), axis=0, keepdims=True)
        for k in range(out_ref.shape[0]):
            out_ref[k, pl.ds(j, 1), :] = peak + jnp.log(total)


def first_kernel(
    me_ref, affinity_ref, firm_ref, *rest
):
    shares, rest = rest[:-8], rest[-8:]
    out_ref, means_ref, projected_ref, rows_ref, kept_ref, peaks_ref, firm_out_ref, scores = rest
    firm_out_ref[...] = firm_ref[...]
    rows_ref[...] = firm_ref[...].astype(BF16)
    for k, part in enumerate(shares):
        rows = part.shape[0]
        begin = pl.multiple_of(jnp.bitwise_xor(me_ref[0], k) * rows, rows)
        means_ref[pl.ds(begin, rows), :] = part[...]
    projected_ref[...] = _dot(means_ref[...].astype(BF16), affinity_ref[...]).astype(BF16)
    for j in range(TILE // WIDE):
        slot = scores.at[j % 2]
        columns = slice(j * WIDE, (j + 1) * WIDE)
        b = projected_ref[columns, :]
        peak = None
        for t in range(TILE // WIDE):
            part = slice(t * WIDE, (t + 1) * WIDE)
            s = _dot(rows_ref[part, :], b, NT)
            slot[part, :] = s
            top = jnp.max(s.reshape(WIDE // 8, 8, WIDE), axis=0)
            peak = top if peak is None else jnp.maximum(peak, top)
        peak = jnp.max(peak, axis=0, keepdims=True)
        total = None
        for t in range(TILE // WIDE):
            part = slice(t * WIDE, (t + 1) * WIDE)
            e = jnp.exp(slot[part, :] - peak)
            kept_ref[part, columns] = e
            e = jnp.sum(e.reshape(WIDE // 8, 8, WIDE), axis=0)
            total = e if total is None else total + e
        lse = peak + jnp.log(jnp.sum(total, axis=0, keepdims=True))
        for i in range(WIDE // LANES):
            line = j * (WIDE // LANES) + i
            peaks_ref[line : line + 1, :] = peak[:, i * LANES : (i + 1) * LANES]
            spread_line(out_ref, line, lse[:, i * LANES : (i + 1) * LANES])


def column_kernel(
    mass, recv_ref, tally_ref, peaks_ref, kept_ref, a_ref, b_ref, out_ref, pot_ref, totals, *spare
):
    pot_ref[...] = combine(recv_ref, tally_ref, mass)
    level = peaks_ref[...] + pot_ref[...]
    top = jnp.max(level, keepdims=True)
    weight = jnp.exp(level - top)
    weights = [weight[t : t + 1, :] for t in range(BLOCKS)]
    for i in range(BLOCKS):
        rows = slice(i * LANES, (i + 1) * LANES)
        total = kept_ref[rows, 0:LANES] * weights[0]
        for t in range(1, BLOCKS):
            total += kept_ref[rows, t * LANES : (t + 1) * LANES] * weights[t]
        totals[i : i + 1, :] = jnp.sum(jnp.transpose(total), axis=0, keepdims=True)
    lse = top + jnp.log(totals[...])
    for k in range(out_ref.shape[0]):
        out_ref[k] = lse

    @pl.when(jnp.min(totals[...]) < TINY)
    def _():
        exact_lse(a_ref, b_ref, pot_ref, *spare, out_ref)


def row_kernel(
    mass, recv_ref, tally_ref, peaks_ref, kept_ref, a_ref, b_ref, out_ref, pot_ref, totals, *spare
):
    pot_ref[...] = combine(recv_ref, tally_ref, mass)
    top = jnp.max(pot_ref[...], keepdims=True)
    weight = jnp.exp(pot_ref[...] - top)
    total = [jnp.zeros((8, LANES), F32)] * BLOCKS
    for i in range(BLOCKS):
        rows = slice(i * LANES, (i + 1) * LANES)
        column = upright(weight[i : i + 1, :])
        for t in range(BLOCKS):
            e = kept_ref[rows, t * LANES : (t + 1) * LANES] * column
            total[t] = total[t] + jnp.sum(e.reshape(LANES // 8, 8, LANES), axis=0)
    for t in range(BLOCKS):
        totals[t : t + 1, :] = jnp.sum(total[t], axis=0, keepdims=True)
    lse = peaks_ref[...] + (top + jnp.log(totals[...]))
    for k in range(out_ref.shape[0]):
        out_ref[k] = lse

    @pl.when(jnp.min(totals[...]) < TINY)
    def _():
        exact_lse(a_ref, b_ref, pot_ref, *spare, out_ref)


def first_pass(me, affinity, firm_rows, shares):
    return pl.pallas_call(
        first_kernel,
        out_shape=(
            pltpu.VMEM((len(shares), BLOCKS, LANES), F32),
            jax.ShapeDtypeStruct((TILE, K), F32),
            jax.ShapeDtypeStruct((TILE, K), BF16),
            jax.ShapeDtypeStruct((TILE, K), BF16),
            pltpu.VMEM((TILE, TILE), F32),
            jax.ShapeDtypeStruct((BLOCKS, LANES), F32),
            jax.ShapeDtypeStruct((TILE, K), F32),
        ),
        in_specs=[SM] + [VM] * (2 + len(shares)),
        out_specs=(VM,) * 7,
        scratch_shapes=[pltpu.VMEM((2, TILE, WIDE), F32)],
        compiler_params=_params(40),
        cost_estimate=LIGHT,
        name="first_pass",
    )(me, affinity, firm_rows, *shares)


def half_sweep(kernel, mass, recv, tally, peaks, kept, a, b, parts):
    small = jax.ShapeDtypeStruct((BLOCKS, LANES), F32)
    return pl.pallas_call(
        functools.partial(kernel, mass),
        out_shape=(pltpu.VMEM((parts, BLOCKS, LANES), F32), small),
        in_specs=[VM] * 4 + [FAR] * 2,
        out_specs=(VM, VM),
        scratch_shapes=[
            pltpu.VMEM((BLOCKS, LANES), F32),
            pltpu.VMEM((TILE, LANES), F32),
            pltpu.VMEM((TILE, LANES), F32),
            pltpu.VMEM((TILE, K), BF16),
            pltpu.VMEM((TILE, K), BF16),
            pltpu.SemaphoreType.DMA((2,)),
        ],
        compiler_params=_params(24),
        cost_estimate=LIGHT,
        name=kernel.__name__,
    )(recv, tally, peaks, kept, _far(a), _far(b))


def last_kernel(mass, recv_ref, tally_ref, pot_ref):
    pot_ref[...] = combine(recv_ref, tally_ref, mass)


def last_pass(mass, recv, tally):
    return pl.pallas_call(
        functools.partial(last_kernel, mass),
        out_shape=jax.ShapeDtypeStruct((BLOCKS, LANES), F32),
        in_specs=[VM] * 2,
        out_specs=VM,
        compiler_params=_params(16),
        cost_estimate=LIGHT,
        name="last_combine",
    )(recv, tally)


def swap(x, axis):
    return lax.all_to_all(x, axis, split_axis=0, concat_axis=0, tiled=True)


def trade(x, axis, s):
    return lax.ppermute(x, axis, [(i, i ^ s) for i in range(lax.axis_size(axis))])


def along_y(parts, axis):
    count = lax.axis_size(axis)
    hop = [(i, (i + 2 - 4 * (i % 2)) % count) for i in range(count)]
    far = lax.ppermute(lax.ppermute(parts[2], axis, hop), axis, hop)
    return [parts[0], trade(parts[1], axis, 2), far, trade(parts[3], axis, 6)]


def records_along_y(parts, axis):
    count = lax.axis_size(axis)
    far = count // 2
    up = lax.ppermute(parts[far], axis, [(i, (i + 2) % count) for i in range(count)])
    down = lax.ppermute(parts[far + 1], axis, [(i, (i - 2) % count) for i in range(count)])
    got = [parts[k] if k == 0 else None for k in range(count)]
    for k in (2, 3, 6, 7):
        got[k] = trade(parts[k], axis, k)
    got[far] = lax.ppermute(up, axis, [(i, (i + 2) % count) for i in range(count)])
    got[far + 1] = lax.ppermute(down, axis, [(i, ((i - 2) % count) ^ 1) for i in range(count)])
    got[1] = trade(parts[1], axis, 1)
    return got


def body(worker_ids, worker_attrs, firm_ids, firm_attrs, affinity):
    wa_count = lax.axis_size("wa")
    af_count = lax.axis_size("af")
    records_all = worker_ids.shape[0] * wa_count * af_count
    wa_me = lax.axis_index("wa").astype(jnp.int32).reshape(1)
    af_me = lax.axis_index("af").astype(jnp.int32).reshape(1)

    worker_sent = pack(worker_ids, worker_attrs, wa_count, None, affinity)
    worker_recv = swap(worker_sent[0], "wa")
    firm_sent = pack(firm_ids, firm_attrs, af_count, af_me, worker_sent[0])
    firm_recv = records_along_y(firm_sent, "af")
    firm_pooled = pool(firm_recv, wa_count, None, [worker_sent[0]])
    firm_part = swap(firm_pooled[0], "wa")
    worker_pooled = pool([worker_recv], af_count, af_me, firm_pooled)
    worker_chip = merge(worker_pooled[0], trade(worker_pooled[1], "af", 1))
    worker_part = along_y(worker_chip, "af")
    firm_mean, firm_tally = mean_share([firm_part], wa_me, True, worker_part[1:])
    firm_means = swap(firm_mean, "wa").reshape(TILE, K)
    worker_mean, worker_tally = mean_share(worker_part, af_me, False, [firm_mean])
    same_core = [worker_mean] + [trade(worker_mean, "af", 2 * k) for k in range(1, af_count // 2)]
    worker_shares = [x for mine in same_core for x in (mine, trade(mine, "af", 1))]

    partial, worker_means, projected, firm_rows, kept, peaks, firm_means = first_pass(
        af_me, affinity, firm_means, worker_shares
    )
    for rounds in range(ITERS):
        partial, worker_potential = half_sweep(
            column_kernel,
            float(records_all + W),
            swap(partial, "af"),
            worker_tally,
            peaks,
            kept,
            projected,
            firm_rows,
            wa_count,
        )
        partial = swap(partial, "wa")
        if rounds < ITERS - 1:
            partial, unused = half_sweep(
                row_kernel,
                float(records_all + F),
                partial,
                firm_tally,
                peaks,
                kept,
                firm_rows,
                projected,
                af_count,
            )
    firm_potential = last_pass(float(records_all + F), partial, firm_tally)
    return (worker_means, firm_means, worker_potential.reshape(TILE), firm_potential.reshape(TILE))


def solution(mesh):
    placed = (P(("wa", "af")), P(("wa", "af"), None), P(("wa", "af")), P(("wa", "af"), None), P())
    return jax.shard_map(
        body,
        mesh=mesh,
        in_specs=placed,
        out_specs=(P("wa", None), P("af", None), P("wa"), P("af")),
        check_vma=False,
    )
```

```python
import functools
import math

import jax
import jax.numpy as jnp
from jax import lax
from jax.experimental import pallas as pl
from jax.experimental.pallas import tpu as pltpu
from jax.sharding import PartitionSpec as P

W = 32768
F = 16384
K = 128
ITERS = 3
TILE = 2048
LANES = 128
BLOCKS = TILE // LANES
ID_ROWS = 16
CHUNK = 512
WIDE = 256
TINY = 1e-25
F32 = jnp.float32
BF16 = jnp.bfloat16

VM = pl.BlockSpec(memory_space=pltpu.VMEM)
SM = pl.BlockSpec(memory_space=pltpu.SMEM)
FAR = pl.BlockSpec(memory_space=pltpu.HBM)
LIGHT = pl.CostEstimate(flops=1 << 20, bytes_accessed=1 << 16, transcendentals=0)
NT = (((1,), (1,)), ((), ()))
NN = (((1,), (0,)), ((), ()))


def _far(x):
    return pltpu.with_memory_space_constraint(x, pltpu.HBM)


def _params(mib):
    return pltpu.CompilerParams(vmem_limit_bytes=mib << 20)


def _dot(a, b, dims=NN):
    return lax.dot_general(a, b, dims, preferred_element_type=F32)


def _flag(mask):
    return jnp.where(mask, 1.0, 0.0).astype(BF16)


def pack_kernel(groups, capacity, me_ref, ids_ref, attrs_ref, after_ref, *rest):
    outs, (dest_v, dest_s, near, wide, placed, sems) = rest[:-6], rest[-6:]
    fetch = pltpu.make_async_copy(attrs_ref, near, sems.at[0])
    fetch.start()
    rows = ids_ref.shape[0]
    ids = ids_ref[...]
    owner = jnp.bitwise_xor(lax.shift_right_logical(ids, 11), me_ref[0])
    local = jnp.bitwise_and(ids, TILE - 1)
    sub = lax.broadcasted_iota(jnp.int32, (LANES, LANES), 0)
    lane = lax.broadcasted_iota(jnp.int32, (LANES, LANES), 1)
    before = _flag(sub < lane)
    every = jnp.ones((LANES, LANES), BF16)
    above = _flag(
        lax.broadcasted_iota(jnp.int32, (rows, rows), 1)
        < lax.broadcasted_iota(jnp.int32, (rows, rows), 0)
    )
    masks = [owner == g for g in range(groups)]
    stacked = jnp.concatenate([_flag(m) for m in masks], axis=0)
    inside = _dot(stacked, before)
    totals = _dot(stacked, every).astype(BF16)
    slot = jnp.zeros((rows, LANES), F32)
    for g in range(groups):
        part = slice(g * rows, (g + 1) * rows)
        slot = jnp.where(masks[g], inside[part] + _dot(above, totals[part]), slot)
    slot = slot.astype(jnp.int32)
    dest_v[...] = owner * capacity + slot
    to_scalar = pltpu.make_async_copy(dest_v, dest_s, sems.at[1])
    to_scalar.start()

    line = lax.shift_right_logical(slot, 7)
    column = jnp.bitwise_and(slot, LANES - 1)
    high_row = owner * ID_ROWS + line
    low_row = high_row + capacity // LANES
    high = (lax.shift_right_logical(local, 6) + 1).astype(F32)
    low = jnp.bitwise_and(local, 63).astype(F32)
    place = lax.broadcasted_iota(jnp.int32, (groups * ID_ROWS, LANES), 0)
    packed = jnp.zeros((groups * ID_ROWS, LANES), F32)
    for c in range(rows):
        r = slice(c, c + 1)
        values = jnp.where(place == high_row[r], high[r], 0.0) + jnp.where(
            place == low_row[r], low[r], 0.0
        )
        packed += _dot(values.astype(BF16), _flag(sub == column[r]), NT)
    packed = packed.astype(BF16)
    for g in range(groups):
        behind = packed[g * ID_ROWS : (g + 1) * ID_ROWS]
        if len(outs) == 1:
            outs[0][g, capacity : capacity + ID_ROWS, :] = behind
        else:
            outs[g][capacity : capacity + ID_ROWS, :] = behind

    placed[...] = jnp.zeros_like(placed)
    fetch.wait()
    wide[...] = near[...].astype(F32)
    to_scalar.wait()

    @pl.loop(0, rows)
    def _(row):
        first = pl.multiple_of(row * LANES, LANES)
        held = [wide[pl.ds(first + u, 1), :] for u in range(LANES)]
        to = [dest_s[row, u] for u in range(LANES)]
        for u in range(LANES):
            placed[pl.ds(to[u], 1), :] = held[u]

    for g in range(groups):
        group = placed[g * capacity : (g + 1) * capacity, :].astype(BF16)
        if len(outs) == 1:
            outs[0][g, 0:capacity, :] = group
        else:
            outs[g][0:capacity, :] = group


def pack(ids, attrs, groups, me, after):
    rows = ids.shape[0]
    capacity = 2 * rows // groups
    if me is None:
        me = jnp.zeros((1,), jnp.int32)
        made = (jax.ShapeDtypeStruct((groups, capacity + ID_ROWS, K), BF16),)
    else:
        made = (jax.ShapeDtypeStruct((capacity + ID_ROWS, K), BF16),) * groups
    return pl.pallas_call(
        functools.partial(pack_kernel, groups, capacity),
        out_shape=made,
        in_specs=[SM, VM, FAR, FAR],
        out_specs=(VM,) * len(made),
        scratch_shapes=[
            pltpu.VMEM((rows // LANES, LANES), jnp.int32),
            pltpu.SMEM((rows // LANES, LANES), jnp.int32),
            pltpu.VMEM((rows, K), BF16),
            pltpu.VMEM((rows, K), F32),
            pltpu.VMEM((groups * capacity, K), F32),
            pltpu.SemaphoreType.DMA((2,)),
        ],
        compiler_params=_params(24),
        cost_estimate=LIGHT,
        name="pack_records",
    )(me, ids.reshape(rows // LANES, LANES), _far(attrs), _far(after))


def pool_kernel(groups, capacity, split, behind, me_ref, *rest):
    recvs, outs, rest = rest[behind : -split - 3], rest[-split - 3 : -3], rest[-3:]
    sums, tallies, more = rest
    if len(recvs) == 1:
        recvs = [recvs[0].at[g] for g in range(groups)]
    half = capacity // 2
    lines = capacity // LANES
    types = lax.broadcasted_iota(jnp.int32, (TILE // 2, CHUNK), 0)

    def ids_of(recv, begin, end):
        coded = recv[capacity : capacity + ID_ROWS, :].astype(F32).astype(jnp.int32)
        return [
            (coded[i : i + 1] - 1) * 64 + coded[lines + i : lines + i + 1]
            for i in range(begin, end)
        ]

    def add(ids, x, fresh=False):
        upper = [
            jnp.where(upright(i.astype(F32)) >= TILE // 2, 1.0, 0.0).astype(BF16) for i in ids
        ]
        high = x * jnp.concatenate(upper, axis=0)
        both = jnp.concatenate([x - high, high], axis=1)
        ids = jnp.concatenate(ids, axis=1)
        wide = ids.shape[1]
        folded = jnp.where(ids >= TILE // 2, ids - TILE // 2, ids)
        total = _dot(_flag(types[:, :wide] == folded), both)
        line = jnp.right_shift(ids, 7)
        column = jnp.bitwise_and(ids, LANES - 1)
        tally = _dot(
            _flag(types[:BLOCKS, :wide] == line), _flag(types[:LANES, :wide] == column), NT
        )
        for side in range(2):
            part = total[:, side * K : (side + 1) * K]
            sums[side] = part if fresh else sums[side] + part
        tallies[...] = tally if fresh else tallies[...] + tally

    for g in range(groups):
        more[g] = jnp.max(
            recvs[g][capacity : capacity + ID_ROWS, :].astype(F32)[lines // 2 : lines]
        ).astype(jnp.int32)
    together = max(1, CHUNK // half)
    for g in range(0, groups, together):
        ids = [i for k in range(together) for i in ids_of(recvs[g + k], 0, lines // 2)]
        x = [recvs[g + k][0:half, :] for k in range(together)]
        add(ids, x[0] if together == 1 else jnp.concatenate(x, axis=0), g == 0)
    for g in range(groups):

        @pl.when(more[g] > 0)
        def _(recv=recvs[g]):
            add(ids_of(recv, lines // 2, lines), recv[half:capacity, :])

    if split == 1:
        parts = outs[0].shape[0]
        share = TILE // parts
        for k in range(parts):
            side, row = divmod(k * share, TILE // 2)
            outs[0][k, 0:share, :] = sums[side, row : row + share, :]
            outs[0][k, share : share + BLOCKS, :] = tallies[...]
        return
    parts = outs[0].shape[0]
    share = TILE // (parts * split)
    for c in range(split):
        for k in range(parts):
            begin = jnp.bitwise_xor(me_ref[0], split * k + c) * share
            side = begin // (TILE // 2)
            row = pl.multiple_of(begin - side * (TILE // 2), share)
            outs[c][k, 0:share, :] = sums[side, pl.ds(row, share), :]
            outs[c][k, share : share + BLOCKS, :] = tallies[...]


def pool(recvs, parts, me, after):
    if len(recvs) == 1:
        groups, depth = recvs[0].shape[:2]
    else:
        groups, depth = len(recvs), recvs[0].shape[0]
    rows = TILE // parts + BLOCKS
    if me is None:
        me = jnp.zeros((1,), jnp.int32)
        made = (jax.ShapeDtypeStruct((parts, rows, K), F32),)
    else:
        made = (jax.ShapeDtypeStruct((parts // 2, rows, K), F32),) * 2
    return pl.pallas_call(
        functools.partial(pool_kernel, groups, depth - ID_ROWS, len(made), len(after)),
        out_shape=made,
        in_specs=[SM] + [FAR] * len(after) + [VM] * len(recvs),
        out_specs=(VM,) * len(made),
        scratch_shapes=[
            pltpu.VMEM((2, TILE // 2, K), F32),
            pltpu.VMEM((BLOCKS, LANES), F32),
            pltpu.SMEM((groups,), jnp.int32),
        ],
        compiler_params=_params(24),
        cost_estimate=LIGHT,
        name="pool_records",
    )(me, *[_far(x) for x in after], *recvs)


def merge_kernel(mine_ref, other_ref, *outs):
    for k, out in enumerate(outs):
        out[...] = mine_ref[k] + other_ref[k]


def merge(mine, other):
    parts, rows, width = mine.shape
    return pl.pallas_call(
        merge_kernel,
        out_shape=(jax.ShapeDtypeStruct((rows, width), F32),) * parts,
        in_specs=[VM, VM],
        out_specs=(VM,) * parts,
        compiler_params=_params(24),
        cost_estimate=LIGHT,
        name="merge_cores",
    )(mine, other)


def upright(row):
    return jnp.transpose(jnp.broadcast_to(row, (LANES, LANES)))


def mean_kernel(share, spread, behind, me_ref, *rest):
    recvs, (mean_ref, tally_ref) = rest[behind:-2], rest[-2:]
    if len(recvs) == 1:
        recvs = [recvs[0].at[k] for k in range(recvs[0].shape[0])]
    tally = recvs[0][share : share + BLOCKS, :]
    total = recvs[0][0:share, :]
    for recv in recvs[1:]:
        tally += recv[share : share + BLOCKS, :]
        total += recv[0:share, :]
    tally_ref[...] = tally
    me = me_ref[0]
    lines = share // LANES
    counts = jnp.concatenate(
        [upright(tally_ref[pl.ds(me * lines + i, 1), :]) for i in range(lines)], axis=0
    )
    means = total / jnp.maximum(counts, 1.0)
    if spread:
        for k in range(len(recvs)):
            mean_ref[k] = means
    else:
        mean_ref[...] = means


def mean_share(recvs, me, spread, after):
    parts = recvs[0].shape[0] if len(recvs) == 1 else len(recvs)
    share = recvs[0].shape[-2] - BLOCKS
    made = jax.ShapeDtypeStruct((parts, share, K) if spread else (share, K), F32)
    return pl.pallas_call(
        functools.partial(mean_kernel, share, spread, len(after)),
        out_shape=(made, jax.ShapeDtypeStruct((BLOCKS, LANES), F32)),
        in_specs=[SM] + [pl.BlockSpec(memory_space=pl.ANY)] * len(after) + [VM] * len(recvs),
        out_specs=(VM,) * 2,
        compiler_params=_params(24),
        cost_estimate=LIGHT,
        name="mean_share",
    )(me, *after, *recvs)


def combine(recv_ref, tally_ref, mass):
    peak = recv_ref[0]
    for k in range(1, recv_ref.shape[0]):
        peak = jnp.maximum(peak, recv_ref[k])
    total = jnp.exp(recv_ref[0] - peak)
    for k in range(1, recv_ref.shape[0]):
        total += jnp.exp(recv_ref[k] - peak)
    return (jnp.log(tally_ref[...] + 1.0) - math.log(mass)) - (peak + jnp.log(total))


def spread_line(out_ref, line, row):
    for k in range(out_ref.shape[0]):
        out_ref[k, line : line + 1, :] = row


def exact_lse(a_far, b_far, pot_ref, shift, scores, a_ref, b_ref, sems, out_ref):
    copies = [
        pltpu.make_async_copy(a_far, a_ref, sems.at[0]),
        pltpu.make_async_copy(b_far, b_ref, sems.at[1]),
    ]
    for copy in copies:
        copy.start()
    for copy in copies:
        copy.wait()
    for i in range(BLOCKS):
        shift[i * LANES : (i + 1) * LANES, :] = upright(pot_ref[i : i + 1, :])

    @pl.loop(0, BLOCKS)
    def _(j):
        b = b_ref[pl.ds(pl.multiple_of(j * LANES, LANES), LANES), :]
        scores[...] = _dot(a_ref[...], b, NT) + shift[...]
        peak = jnp.max(scores[...], axis=0, keepdims=True)
        total = jnp.sum(jnp.exp(scores[...] - peak), axis=0, keepdims=True)
        for k in range(out_ref.shape[0]):
            out_ref[k, pl.ds(j, 1), :] = peak + jnp.log(total)


def first_kernel(
    me_ref, affinity_ref, firm_ref, *rest
):
    shares, rest = rest[:-8], rest[-8:]
    out_ref, means_ref, projected_ref, rows_ref, kept_ref, peaks_ref, firm_out_ref, scores = rest
    firm_out_ref[...] = firm_ref[...]
    rows_ref[...] = firm_ref[...].astype(BF16)
    for k, part in enumerate(shares):
        rows = part.shape[0]
        begin = pl.multiple_of(jnp.bitwise_xor(me_ref[0], k) * rows, rows)
        means_ref[pl.ds(begin, rows), :] = part[...]
    projected_ref[...] = _dot(means_ref[...].astype(BF16), affinity_ref[...]).astype(BF16)
    for j in range(TILE // WIDE):
        slot = scores.at[j % 2]
        columns = slice(j * WIDE, (j + 1) * WIDE)
        b = projected_ref[columns, :]
        peak = None
        for t in range(TILE // WIDE):
            part = slice(t * WIDE, (t + 1) * WIDE)
            s = _dot(rows_ref[part, :], b, NT)
            slot[part, :] = s
            top = jnp.max(s.reshape(WIDE // 8, 8, WIDE), axis=0)
            peak = top if peak is None else jnp.maximum(peak, top)
        peak = jnp.max(peak, axis=0, keepdims=True)
        total = None
        for t in range(TILE // WIDE):
            part = slice(t * WIDE, (t + 1) * WIDE)
            e = jnp.exp(slot[part, :] - peak)
            kept_ref[part, columns] = e
            e = jnp.sum(e.reshape(WIDE // 8, 8, WIDE), axis=0)
            total = e if total is None else total + e
        lse = peak + jnp.log(jnp.sum(total, axis=0, keepdims=True))
        for i in range(WIDE // LANES):
            line = j * (WIDE // LANES) + i
            peaks_ref[line : line + 1, :] = peak[:, i * LANES : (i + 1) * LANES]
            spread_line(out_ref, line, lse[:, i * LANES : (i + 1) * LANES])


def column_kernel(
    mass, recv_ref, tally_ref, peaks_ref, kept_ref, a_ref, b_ref, out_ref, pot_ref, totals, *spare
):
    pot_ref[...] = combine(recv_ref, tally_ref, mass)
    level = peaks_ref[...] + pot_ref[...]
    top = jnp.max(level, keepdims=True)
    weight = jnp.exp(level - top)
    weights = [weight[t : t + 1, :] for t in range(BLOCKS)]
    for i in range(BLOCKS):
        rows = slice(i * LANES, (i + 1) * LANES)
        total = kept_ref[rows, 0:LANES] * weights[0]
        for t in range(1, BLOCKS):
            total += kept_ref[rows, t * LANES : (t + 1) * LANES] * weights[t]
        totals[i : i + 1, :] = jnp.sum(jnp.transpose(total), axis=0, keepdims=True)
    lse = top + jnp.log(totals[...])
    for k in range(out_ref.shape[0]):
        out_ref[k] = lse

    @pl.when(jnp.min(totals[...]) < TINY)
    def _():
        exact_lse(a_ref, b_ref, pot_ref, *spare, out_ref)


def row_kernel(
    mass, recv_ref, tally_ref, peaks_ref, kept_ref, a_ref, b_ref, out_ref, pot_ref, totals, *spare
):
    pot_ref[...] = combine(recv_ref, tally_ref, mass)
    top = jnp.max(pot_ref[...], keepdims=True)
    weight = jnp.exp(pot_ref[...] - top)
    total = [jnp.zeros((8, LANES), F32)] * BLOCKS
    for i in range(BLOCKS):
        rows = slice(i * LANES, (i + 1) * LANES)
        column = upright(weight[i : i + 1, :])
        for t in range(BLOCKS):
            e = kept_ref[rows, t * LANES : (t + 1) * LANES] * column
            total[t] = total[t] + jnp.sum(e.reshape(LANES // 8, 8, LANES), axis=0)
    for t in range(BLOCKS):
        totals[t : t + 1, :] = jnp.sum(total[t], axis=0, keepdims=True)
    lse = peaks_ref[...] + (top + jnp.log(totals[...]))
    for k in range(out_ref.shape[0]):
        out_ref[k] = lse

    @pl.when(jnp.min(totals[...]) < TINY)
    def _():
        exact_lse(a_ref, b_ref, pot_ref, *spare, out_ref)


def first_pass(me, affinity, firm_rows, shares):
    return pl.pallas_call(
        first_kernel,
        out_shape=(
            pltpu.VMEM((len(shares), BLOCKS, LANES), F32),
            jax.ShapeDtypeStruct((TILE, K), F32),
            jax.ShapeDtypeStruct((TILE, K), BF16),
            jax.ShapeDtypeStruct((TILE, K), BF16),
            pltpu.VMEM((TILE, TILE), F32),
            jax.ShapeDtypeStruct((BLOCKS, LANES), F32),
            jax.ShapeDtypeStruct((TILE, K), F32),
        ),
        in_specs=[SM] + [VM] * (2 + len(shares)),
        out_specs=(VM,) * 7,
        scratch_shapes=[pltpu.VMEM((2, TILE, WIDE), F32)],
        compiler_params=_params(40),
        cost_estimate=LIGHT,
        name="first_pass",
    )(me, affinity, pltpu.with_memory_space_constraint(firm_rows, pltpu.VMEM), *shares)


def half_sweep(kernel, mass, recv, tally, peaks, kept, a, b, parts):
    small = jax.ShapeDtypeStruct((BLOCKS, LANES), F32)
    return pl.pallas_call(
        functools.partial(kernel, mass),
        out_shape=(pltpu.VMEM((parts, BLOCKS, LANES), F32), small),
        in_specs=[VM] * 4 + [FAR] * 2,
        out_specs=(VM, VM),
        scratch_shapes=[
            pltpu.VMEM((BLOCKS, LANES), F32),
            pltpu.VMEM((TILE, LANES), F32),
            pltpu.VMEM((TILE, LANES), F32),
            pltpu.VMEM((TILE, K), BF16),
            pltpu.VMEM((TILE, K), BF16),
            pltpu.SemaphoreType.DMA((2,)),
        ],
        compiler_params=_params(24),
        cost_estimate=LIGHT,
        name=kernel.__name__,
    )(recv, tally, peaks, kept, _far(a), _far(b))


def last_kernel(mass, recv_ref, tally_ref, pot_ref):
    pot_ref[...] = combine(recv_ref, tally_ref, mass)


def last_pass(mass, recv, tally):
    return pl.pallas_call(
        functools.partial(last_kernel, mass),
        out_shape=jax.ShapeDtypeStruct((BLOCKS, LANES), F32),
        in_specs=[VM] * 2,
        out_specs=VM,
        compiler_params=_params(16),
        cost_estimate=LIGHT,
        name="last_combine",
    )(recv, tally)


def swap(x, axis):
    return lax.all_to_all(x, axis, split_axis=0, concat_axis=0, tiled=True)


def trade(x, axis, s):
    return lax.ppermute(x, axis, [(i, i ^ s) for i in range(lax.axis_size(axis))])


def along_y(parts, axis):
    count = lax.axis_size(axis)
    hop = [(i, (i + 2 - 4 * (i % 2)) % count) for i in range(count)]
    far = lax.ppermute(lax.ppermute(parts[2], axis, hop), axis, hop)
    return [parts[0], trade(parts[1], axis, 2), far, trade(parts[3], axis, 6)]


def records_along_y(parts, axis):
    count = lax.axis_size(axis)
    far = count // 2
    up = lax.ppermute(parts[far], axis, [(i, (i + 2) % count) for i in range(count)])
    down = lax.ppermute(parts[far + 1], axis, [(i, (i - 2) % count) for i in range(count)])
    got = [parts[k] if k == 0 else None for k in range(count)]
    for k in (2, 3, 6, 7):
        got[k] = trade(parts[k], axis, k)
    got[far] = lax.ppermute(up, axis, [(i, (i + 2) % count) for i in range(count)])
    got[far + 1] = lax.ppermute(down, axis, [(i, ((i - 2) % count) ^ 1) for i in range(count)])
    got[1] = trade(parts[1], axis, 1)
    return got


def body(worker_ids, worker_attrs, firm_ids, firm_attrs, affinity):
    wa_count = lax.axis_size("wa")
    af_count = lax.axis_size("af")
    records_all = worker_ids.shape[0] * wa_count * af_count
    wa_me = lax.axis_index("wa").astype(jnp.int32).reshape(1)
    af_me = lax.axis_index("af").astype(jnp.int32).reshape(1)

    worker_sent = pack(worker_ids, worker_attrs, wa_count, None, affinity)
    worker_recv = swap(worker_sent[0], "wa")
    firm_sent = pack(firm_ids, firm_attrs, af_count, af_me, worker_sent[0])
    firm_recv = records_along_y(firm_sent, "af")
    firm_pooled = pool(firm_recv, wa_count, None, [worker_sent[0]])
    firm_part = swap(firm_pooled[0], "wa")
    worker_pooled = pool([worker_recv], af_count, af_me, firm_pooled)
    worker_chip = merge(worker_pooled[0], trade(worker_pooled[1], "af", 1))
    worker_part = along_y(worker_chip, "af")
    firm_mean, firm_tally = mean_share([firm_part], wa_me, True, worker_part[1:])
    firm_means = swap(firm_mean, "wa").reshape(TILE, K)
    worker_mean, worker_tally = mean_share(worker_part, af_me, False, [firm_mean])
    same_core = [worker_mean] + [trade(worker_mean, "af", 2 * k) for k in range(1, af_count // 2)]
    worker_shares = [x for mine in same_core for x in (mine, trade(mine, "af", 1))]

    partial, worker_means, projected, firm_rows, kept, peaks, firm_means = first_pass(
        af_me, affinity, firm_means, worker_shares
    )
    for rounds in range(ITERS):
        partial, worker_potential = half_sweep(
            column_kernel,
            float(records_all + W),
            swap(partial, "af"),
            worker_tally,
            peaks,
            kept,
            projected,
            firm_rows,
            wa_count,
        )
        partial = swap(partial, "wa")
        if rounds < ITERS - 1:
            partial, unused = half_sweep(
                row_kernel,
                float(records_all + F),
                partial,
                firm_tally,
                peaks,
                kept,
                firm_rows,
                projected,
                af_count,
            )
    firm_potential = last_pass(float(records_all + F), partial, firm_tally)
    return (worker_means, firm_means, worker_potential.reshape(TILE), firm_potential.reshape(TILE))


def solution(mesh):
    placed = (P(("wa", "af")), P(("wa", "af"), None), P(("wa", "af")), P(("wa", "af"), None), P())
    return jax.shard_map(
        body,
        mesh=mesh,
        in_specs=placed,
        out_specs=(P("wa", None), P("af", None), P("wa"), P("af")),
        check_vma=False,
    )
```
